512 devices in a mesh: adapter: 32 (over x, z), tensor: 16 (over y, core).
Axes of the slice: x: 4, y: 8, z: 8, core: 2. Of those that a mesh axis runs over, the one named last changes fastest.
Arguments:
- tokens: bfloat16 [32768, 8192], P('adapter', 'tensor'), may hold values from -6 to 6
- row_adapter_index: int32 [32768, 1], P('adapter'), may hold values from 0 to 511; in each aligned block of 1024 rows (0 to 1023, 1024 to 2047, ...) at most 4 rows name the same one
- adapter_down_weight: bfloat16 [512, 8192, 64], P('adapter', 'tensor'), may hold values from -0.0625 to 0.0625
- adapter_up_weight: bfloat16 [512, 64, 2048], P('adapter', None, 'tensor'), may hold values from -0.75 to 0.75
- key_value_weight: bfloat16 [8192, 2048], P('tensor'), may hold values from -0.09375 to 0.09375
- accepted_branch_rows: int32 [32, 32, 4], P('adapter'), may hold values from 0 to 1023, as said below
- owner_cache_slots: int32 [32, 32, 4], P(None, 'adapter'), may hold values from 0 to 127, as said below
Outputs:
- key_value: bfloat16 [32768, 2048], P('adapter', 'tensor')
- decode_cache: bfloat16 [4096, 2048], P('adapter', 'tensor')
The draws below stay inside these ranges and needn't reach their ends.
Inputs may be any that keep to these rules, and one draw needn't show every extreme that they name: `row_adapter_index`: among the rows of one device no adapter is named by more than 4 rows; in the rows of some device some adapter is named by exactly 4. For each s the 128 entries accepted_branch_rows[s] are distinct. For each owner o the entries owner_cache_slots[:, o, :] name every slot of 0 to 127 once.
All inputs are finite; a program needn't handle non-finite values.
Results may differ from the reference program's by a relative error of at most 0.025.
Values may be sent and summed in bfloat16 or wider, within the bound.
No kernel may reach another device: no remote copies, remote signals or barrier semaphores. Data moves between devices by JAX's collectives and lax.ppermute only.
A program may use at most 64 MiB of HBM per device.

```python
import math
import jax
import jax.numpy as jnp
import numpy as np
from jax import lax

MODEL_WIDTH = 8192
ADAPTER_COUNT = 512
ADAPTER_RANK = 64
CAP = 4
TOK_DEV = 1024
ACC_PEER = 4
KV_COLUMNS = 2048
TOKENS = 32768
ACCEPT = 128
N_TENSOR = 16


def pick_rows(subkey):
    return jax.random.permutation(subkey, TOK_DEV)[:ACCEPT]


def pick_order(subkey):
    return jax.random.permutation(subkey, ACCEPT)


def draw_accepted_branch_rows(key, part):
    number = ACCEPT // ACC_PEER
    subkeys = jax.random.split(jax.random.fold_in(key, 11), number)
    chosen = jax.vmap(pick_rows)(subkeys)
    return chosen.reshape(number, number, ACC_PEER).astype(jnp.int32)


def draw_owner_cache_slots(key, part):
    number = ACCEPT // ACC_PEER
    subkeys = jax.random.split(jax.random.fold_in(key, 23), number)
    orders = jax.vmap(pick_order)(subkeys)
    return jnp.transpose(orders.reshape(number, number, ACC_PEER), (1, 0, 2)).astype(jnp.int32)


def spiked(array, rng, source, target, shards_of, factor):
    def block_of(axis_at):
        return (jnp.arange(array.shape[axis_at]) // (array.shape[axis_at] // shards_of)).reshape((-1,) + (1,) * (array.ndim - 1 - axis_at))

    first = jax.random.permutation(rng, shards_of)[block_of(target)]
    other_side = (block_of(target) + shards_of // 2) % shards_of
    return jnp.where((block_of(source) == first) | (block_of(source) == other_side), factor * array, array)


def levels(own_key, shape, pieces, least, top_value):
    level, own = 1.0, jax.random.fold_in(own_key, 6)
    for dim, blocks in pieces:
        draws = jnp.exp(jax.random.uniform(jax.random.fold_in(own, dim), (blocks,), jnp.float32, least / len(pieces), top_value / len(pieces)))
        level = level * jnp.repeat(draws, shape[dim] // blocks).reshape([-1 if axis == dim else 1 for axis in range(len(shape))])
    return level


def shared_out(rng, own, number, rows, amount, top, reach, skew):
    sequence = jax.random.permutation(rng, amount)
    packed, usual = load_shares(amount, rows * top, reach, skew, True), load_shares(amount, rows * top, reach, skew, False)
    places = jnp.arange(amount)

    def named(lengths, rotation):
        used = int((lengths > 0).sum())
        fixed = max(1, used // 4)
        shifted = fixed + (places - fixed + rotation * (used - fixed)) % max(1, amount - fixed)
        return jnp.zeros((amount,), jnp.int32).at[sequence[jnp.where(places < fixed, places, shifted)]].set(jnp.asarray(lengths, jnp.int32))

    lengths = jnp.where(number % 4 == 0, named(packed, number // 4), named(usual, number - number // 4 - 1))
    mixed = jax.random.permutation(jax.random.fold_in(own, 3), amount)
    source_of, receiver = mixed[0:amount // 2 * 2:2], mixed[1:amount // 2 * 2:2]
    slack = jnp.minimum(lengths[source_of] - 1, reach - lengths[receiver]) // 2
    slack = jnp.where((source_of == sequence[0]) | (receiver == sequence[0]) | (lengths[receiver] == 0), 0, jnp.maximum(slack, 0))
    shifted = jax.random.randint(jax.random.fold_in(own, 4), (amount // 2,), 0, 1 << 20) % (slack + 1)
    lengths = lengths.at[source_of].add(-shifted).at[receiver].add(shifted)
    members = jnp.searchsorted(jnp.cumsum(lengths), jnp.arange(rows * top), side="right").astype(jnp.int32)
    listing = members.reshape(top, rows).T
    listing = listing[jax.random.permutation(jax.random.fold_in(own, 1), rows)]
    rotation = jax.random.randint(jax.random.fold_in(own, 2), (rows, 1), 0, top)
    return jnp.take_along_axis(listing, (jnp.arange(top)[None, :] + rotation) % top, axis=1)


def load_shares(count, total, most, slope, full):
    loads = [(1 << 20) // math.isqrt(grade ** slope) + 1 for grade in range(1, count + 1)]
    largest = most if full else min(most, max(-(-total // count), total * loads[0] // sum(loads)))
    least = 1 if total - largest >= count - 1 else 0
    holding, spare = [largest] + [least] * (count - 1), total - largest - least * (count - 1)
    while spare > 0:
        candidates = [i for i in range(1, count) if holding[i] < largest] or [i for i in range(1, count) if holding[i] < most]
        mass, budget = sum([loads[i] for i in candidates]), spare
        for i in candidates:
            more = min(most - holding[i], max(1, budget * loads[i] // mass), spare)
            holding[i] = holding[i] + more
            spare = spare - more
    return np.array(holding)


def noise(stream_key, dims, width, bound, cuts=(), held_as=jnp.bfloat16):
    entries = width * jax.random.normal(stream_key, dims, jnp.float32)
    if cuts:
        entries = entries * levels(stream_key, dims, cuts, -0.22, 0.18)
    return jnp.clip(entries, -bound, bound).astype(held_as)


def heavy_noise(stream_key, shape, width, reach, shards, heavy, held_as=jnp.bfloat16):
    result = width * jax.random.normal(stream_key, shape, jnp.float32)
    if shards:
        result = result * levels(stream_key, shape, shards, -0.22, 0.18)
    return jnp.clip(spiked(result, jax.random.fold_in(stream_key, 3), *heavy), -reach, reach).astype(held_as)


def setup_inputs(seed: int = 0) -> dict:
    arg_keys = jax.random.split(jax.random.key(seed), 8)
    tokens = noise(arg_keys[0], (TOKENS, MODEL_WIDTH), 1.0, 6.0, ((0, 32), (1, 16)))
    row_adapter_index_keys = jax.random.split(jax.random.fold_in(arg_keys[1], 1), TOKENS // TOK_DEV)
    row_adapter_index_turns = jax.random.permutation(jax.random.fold_in(arg_keys[1], 3), TOKENS // TOK_DEV)
    row_adapter_index = jax.vmap(lambda own, number: shared_out(jax.random.fold_in(arg_keys[1], 2), own, number, TOK_DEV, ADAPTER_COUNT, 1, CAP, 2))(row_adapter_index_keys, row_adapter_index_turns).reshape((TOKENS, 1))
    adapter_down_weight = noise(arg_keys[2], (ADAPTER_COUNT, MODEL_WIDTH, ADAPTER_RANK), MODEL_WIDTH ** -0.5, 0.0625, ((0, 32), (1, 16)))
    adapter_up_weight = noise(arg_keys[3], (ADAPTER_COUNT, ADAPTER_RANK, KV_COLUMNS), ADAPTER_RANK ** -0.5, 0.75, ((0, 32), (2, 16)))
    key_value_weight = heavy_noise(arg_keys[4], (MODEL_WIDTH, KV_COLUMNS), MODEL_WIDTH ** -0.5, 0.09375, ((0, 16),), (0, 1, 16, 2.0))
    accepted_branch_rows = draw_accepted_branch_rows(jax.random.fold_in(arg_keys[7], 71), 0)
    owner_cache_slots = draw_owner_cache_slots(jax.random.fold_in(arg_keys[7], 71), 0)
    return {"tokens": tokens, "row_adapter_index": row_adapter_index, "adapter_down_weight": adapter_down_weight, "adapter_up_weight": adapter_up_weight, "key_value_weight": key_value_weight, "accepted_branch_rows": accepted_branch_rows, "owner_cache_slots": owner_cache_slots}


def block_ranks(labels):
    position = jnp.arange(labels.shape[0], dtype=jnp.int32)
    matching = (labels[:, None] == labels[None, :]) & (position[:, None] > position[None, :])
    return jnp.sum(matching.astype(jnp.int32), axis=1)


def single_adapter(operands):
    gathered, down_weight, up_weight = operands
    flat_rows = gathered.reshape(gathered.shape[0] * gathered.shape[1], gathered.shape[2])
    lowered = jnp.dot(flat_rows, down_weight, preferred_element_type=jnp.float32).astype(jnp.bfloat16)
    return jnp.dot(lowered, up_weight, preferred_element_type=jnp.float32).astype(jnp.bfloat16)


def reference(tokens, row_adapter_index, adapter_down_weight, adapter_up_weight, key_value_weight, accepted_branch_rows, owner_cache_slots):
    sources = TOKENS // TOK_DEV
    shard_width = MODEL_WIDTH // N_TENSOR
    base = jnp.zeros((TOKENS, KV_COLUMNS), jnp.float32)
    for shard in range(N_TENSOR):
        lower = shard * shard_width
        piece = jnp.dot(tokens[:, lower:lower + shard_width], key_value_weight[lower:lower + shard_width, :], preferred_element_type=jnp.float32).astype(jnp.bfloat16)
        piece = lax.optimization_barrier(piece)
        base = base + piece.astype(jnp.float32)
    labels = row_adapter_index[:, 0].reshape(sources, TOK_DEV).astype(jnp.int32)
    ranks = jax.vmap(block_ranks)(labels).astype(jnp.int32)
    blocks = jnp.broadcast_to(jnp.arange(sources, dtype=jnp.int32)[:, None], (sources, TOK_DEV))
    packed_rows = jnp.zeros((ADAPTER_COUNT, sources, CAP, MODEL_WIDTH), jnp.bfloat16)
    packed_rows = packed_rows.at[labels, blocks, ranks].set(tokens.reshape(sources, TOK_DEV, MODEL_WIDTH))
    cache_updates = lax.map(single_adapter, (packed_rows, adapter_down_weight, adapter_up_weight))
    update_row_block = cache_updates[labels, blocks * CAP + ranks]
    key_value = (base + update_row_block.reshape(TOKENS, KV_COLUMNS).astype(jnp.float32)).astype(jnp.bfloat16)
    source_index = jnp.arange(sources, dtype=jnp.int32)[:, None, None]
    owner_index = jnp.arange(sources, dtype=jnp.int32)[None, :, None]
    global_rows = (source_index * TOK_DEV + accepted_branch_rows).reshape(-1).astype(jnp.int32)
    targets = (owner_index * ACCEPT + owner_cache_slots).reshape(-1).astype(jnp.int32)
    decode_cache = jnp.zeros((sources * ACCEPT, KV_COLUMNS), jnp.bfloat16).at[targets].set(key_value[global_rows])
    return key_value, decode_cache
```

```python
import functools

import jax
import jax.numpy as jnp
from jax import lax
from jax.experimental import pallas as pl
from jax.experimental.pallas import tpu as pltpu
from jax.sharding import PartitionSpec as P

ADAPTER_COUNT = 512
CAP = 4
QUAD = 4
VMEM = pl.BlockSpec(memory_space=pltpu.VMEM)
LIMIT = 20 * 1024 * 1024
BF16 = jnp.bfloat16
F32 = jnp.float32


def call(kernel, out_shape, operands, flops, scratch=(), name=None):
    outs = out_shape if isinstance(out_shape, (list, tuple)) else [out_shape]
    size = sum(x.size * x.dtype.itemsize for x in list(operands) + list(outs))
    return pl.pallas_call(
        kernel,
        out_shape=out_shape,
        in_specs=[VMEM] * len(operands),
        out_specs=jax.tree.map(lambda _: VMEM, out_shape),
        scratch_shapes=list(scratch),
        compiler_params=pltpu.CompilerParams(vmem_limit_bytes=LIMIT),
        cost_estimate=pl.CostEstimate(flops=flops, bytes_accessed=size, transcendentals=0),
        name=name,
    )(*operands)


def base_kernel(columns, tokens_ref, weight_ref, out_ref):
    product = jnp.dot(tokens_ref[...], weight_ref[...], preferred_element_type=F32).astype(BF16)
    for part in range(out_ref.shape[0]):
        out_ref[part] = product[:, part * columns : (part + 1) * columns]


def partial_base(tokens, weight, groups):
    rows, features = tokens.shape
    columns = weight.shape[1] // groups
    step = 4
    return pl.pallas_call(
        functools.partial(base_kernel, columns),
        grid=(groups // step,),
        in_specs=[
            pl.BlockSpec((rows, features), lambda i: (0, 0)),
            pl.BlockSpec((features, step * columns), lambda i: (0, i)),
        ],
        out_specs=pl.BlockSpec((step, rows, columns), lambda i: (i, 0, 0)),
        out_shape=jax.ShapeDtypeStruct((groups, rows, columns), BF16),
        compiler_params=pltpu.CompilerParams(vmem_limit_bytes=LIMIT),
        cost_estimate=pl.CostEstimate(
            flops=2 * rows * features * groups * columns,
            bytes_accessed=2 * (rows * features + (features + rows) * groups * columns),
            transcendentals=0,
        ),
        name="base",
    )(tokens, weight)


def pack_kernel(labels_ref, tokens_ref, slots_ref, packed_ref):
    rows = tokens_ref.shape[0]
    labels = labels_ref[...]
    column = jnp.transpose(jnp.broadcast_to(labels, (8, rows)))[:, 0:1]
    earlier = lax.broadcasted_iota(jnp.int32, (rows, rows), 0) < lax.broadcasted_iota(
        jnp.int32, (rows, rows), 1
    )
    same = jnp.where((column == labels) & earlier, 1, 0)
    slots = labels * CAP + jnp.sum(same, axis=0, keepdims=True)
    slots_ref[...] = slots
    tokens = tokens_ref[...]
    block = 256

    @pl.loop(0, packed_ref.shape[0] // block)
    def _(i):
        first = pl.multiple_of(i * block, block)
        place = lax.broadcasted_iota(jnp.int32, (block, rows), 0) + first
        chosen = jnp.where(place == slots, 1.0, 0.0).astype(BF16)
        packed_ref[pl.ds(first, block), :] = jnp.dot(
            chosen, tokens, preferred_element_type=F32
        ).astype(BF16)


def pack(labels, tokens):
    rows, features = tokens.shape
    slots = ADAPTER_COUNT * CAP
    return call(
        pack_kernel,
        [
            jax.ShapeDtypeStruct((1, rows), jnp.int32),
            jax.ShapeDtypeStruct((slots, features), BF16),
        ],
        (labels, tokens),
        2 * slots * rows * features,
        name="pack",
    )


def down_kernel(rows_ref, weight_ref, out_ref):
    sources, slots, features = rows_ref.shape
    rank = weight_ref.shape[1]
    tile = QUAD * CAP
    owner = lax.broadcasted_iota(jnp.int32, (1, tile, 1), 1) // CAP
    for quad in range(slots // tile):
        rows = rows_ref[:, quad * tile : (quad + 1) * tile, :].reshape(sources * tile, features)
        weight = weight_ref[quad * QUAD : (quad + 1) * QUAD].reshape(QUAD * rank, features)
        product = lax.dot_general(
            rows, weight, (((1,), (1,)), ((), ())), preferred_element_type=F32
        ).reshape(sources, tile, QUAD * rank)
        lowered = jnp.zeros((sources, tile, rank), F32)
        for k in range(QUAD):
            lowered = jnp.where(owner == k, product[:, :, k * rank : (k + 1) * rank], lowered)
        lowered = lowered.reshape(sources // 2, 2, tile, rank)
        out_ref[:, quad * tile : (quad + 1) * tile, :] = jnp.concatenate(
            [lowered[:, 0], lowered[:, 1]], axis=-1
        ).astype(BF16)


def lower(received, weight):
    sources, slots, features = received.shape
    rank = weight.shape[1]
    return call(
        down_kernel,
        jax.ShapeDtypeStruct((sources // 2, slots, 2 * rank), BF16),
        (received, weight),
        2 * sources * slots * features * rank * QUAD,
        name="down",
    )


def up_kernel(lowered_ref, weight_ref, out_ref):
    pairs, slots, wide = lowered_ref.shape
    rank = wide // 2
    tile = QUAD * CAP
    columns = weight_ref.shape[2]
    shape = (pairs, tile, QUAD * rank)
    owner = lax.broadcasted_iota(jnp.int32, shape, 1) // CAP
    lane = lax.broadcasted_iota(jnp.int32, shape, 2) // rank
    own = (owner == lane).reshape(pairs * tile, QUAD * rank)
    for quad in range(slots // tile):
        both = lowered_ref[:, quad * tile : (quad + 1) * tile, :].reshape(pairs * tile, wide)
        weight = weight_ref[quad * QUAD : (quad + 1) * QUAD].reshape(QUAD * rank, columns)
        for half in range(2):
            lowered = both[:, half * rank : (half + 1) * rank]
            spread = jnp.where(own, jnp.concatenate([lowered] * QUAD, axis=-1), 0)
            out_ref[:, half, quad * tile : (quad + 1) * tile, :] = (
                jnp.dot(spread.astype(BF16), weight, preferred_element_type=F32)
                .astype(BF16)
                .reshape(pairs, tile, columns)
            )


def raise_rank(lowered, weight):
    pairs, slots, wide = lowered.shape
    columns = weight.shape[2]
    return call(
        up_kernel,
        jax.ShapeDtypeStruct((pairs, 2, slots, columns), BF16),
        (lowered, weight),
        pairs * 2 * slots * columns * wide * QUAD,
        name="up",
    )


def unpack_kernel(slots_ref, out_ref):
    rows, places = out_ref.shape
    slots = slots_ref[...]
    column = jnp.transpose(jnp.broadcast_to(slots, (8, rows)))[:, 0:1]
    block = 256
    for first in range(0, places, block):
        place = lax.broadcasted_iota(jnp.int32, (rows, block), 1) + first
        out_ref[:, first : first + block] = jnp.where(place == column, 1.0, 0.0).astype(BF16)


def finish_kernel(take_ref, returned_ref, base_ref, accepted_ref, out_ref, chosen_ref):
    rows = base_ref.shape[0]
    update = jnp.dot(take_ref[...], returned_ref[...], preferred_element_type=F32)
    key_value = (base_ref[...].astype(F32) + update).astype(BF16)
    out_ref[...] = key_value
    count = chosen_ref.shape[0]
    place = lax.broadcasted_iota(jnp.int32, (count, rows), 1)
    column = jnp.transpose(jnp.broadcast_to(accepted_ref[...], (8, count)))[:, 0:1]
    take = jnp.where(place == column, 1.0, 0.0).astype(BF16)
    chosen_ref[...] = jnp.dot(take, key_value, preferred_element_type=F32).astype(BF16)


def cache_kernel(targets_ref, moved_ref, out_ref):
    count = targets_ref.shape[1]
    place = lax.broadcasted_iota(jnp.int32, (out_ref.shape[0], count), 0)
    take = jnp.where(place == targets_ref[...], 1.0, 0.0).astype(BF16)
    out_ref[...] = jnp.dot(take, moved_ref[...], preferred_element_type=F32).astype(BF16)


def exchange(array, axis):
    return lax.all_to_all(array, axis, split_axis=0, concat_axis=0, tiled=True)


def per_device(
    tokens,
    row_adapter_index,
    adapter_down_weight,
    adapter_up_weight,
    key_value_weight,
    accepted_branch_rows,
    owner_cache_slots,
):
    owners, groups = lax.axis_size("adapter"), lax.axis_size("tensor")
    rows, features = tokens.shape
    columns = adapter_up_weight.shape[2]
    resident = adapter_down_weight.shape[0]
    here = resident * CAP

    partial_sum = partial_base(tokens, key_value_weight, groups).reshape(groups * rows, columns)
    base = lax.psum_scatter(partial_sum, "tensor", scatter_dimension=0, tiled=True)

    row_adapter_index, _ = lax.optimization_barrier((row_adapter_index, partial_sum))
    slots, packed = pack(row_adapter_index.reshape(1, rows), tokens)
    received = exchange(packed.reshape(owners, here, features), "adapter")
    partial_rank = lower(received, jnp.swapaxes(adapter_down_weight, 1, 2))
    pieces = exchange(partial_rank, "tensor")
    summed = jnp.sum(pieces.astype(F32), axis=0).astype(BF16)
    lowered = lax.all_gather(summed, "tensor", axis=0, tiled=False)
    update = raise_rank(lowered, adapter_up_weight)
    returned = exchange(update.reshape(owners, here, columns), "adapter")
    take = call(
        unpack_kernel, jax.ShapeDtypeStruct((rows, owners * here), BF16), (slots,), 0, name="unpack"
    )
    accepted = accepted_branch_rows.reshape(1, -1)
    count = accepted.shape[1]
    key_value, chosen = call(
        finish_kernel,
        [
            jax.ShapeDtypeStruct((rows, columns), BF16),
            jax.ShapeDtypeStruct((count, columns), BF16),
        ],
        (take, returned.reshape(owners * here, columns), base, accepted),
        2 * rows * owners * here * columns,
        name="finish",
    )
    moved = exchange(chosen.reshape(owners, -1, columns), "adapter").reshape(-1, columns)
    decode_cache = call(
        cache_kernel,
        jax.ShapeDtypeStruct((moved.shape[0], columns), BF16),
        (owner_cache_slots.reshape(1, -1), moved),
        2 * count * count * columns,
        name="cache",
    )
    return (key_value, decode_cache)


def solution(mesh):
    in_specs = (
        P("adapter", "tensor"),
        P("adapter", None),
        P("adapter", "tensor", None),
        P("adapter", None, "tensor"),
        P("tensor", None),
        P("adapter", None, None),
        P(None, "adapter", None),
    )
    out_specs = (P("adapter", "tensor"), P("adapter", "tensor"))
    return jax.shard_map(
        per_device, mesh=mesh, in_specs=in_specs, out_specs=out_specs, check_vma=False
    )
```

```python
import functools

import jax
import jax.numpy as jnp
from jax import lax
from jax.experimental import pallas as pl
from jax.experimental.pallas import tpu as pltpu
from jax.sharding import PartitionSpec as P

ADAPTER_COUNT = 512
CAP = 4
QUAD = 4
VMEM = pl.BlockSpec(memory_space=pltpu.VMEM)
LIMIT = 20 * 1024 * 1024
BF16 = jnp.bfloat16
F32 = jnp.float32


def call(kernel, out_shape, operands, flops, scratch=(), name=None):
    outs = out_shape if isinstance(out_shape, (list, tuple)) else [out_shape]
    size = sum(x.size * x.dtype.itemsize for x in list(operands) + list(outs))
    return pl.pallas_call(
        kernel,
        out_shape=out_shape,
        in_specs=[VMEM] * len(operands),
        out_specs=jax.tree.map(lambda _: VMEM, out_shape),
        scratch_shapes=list(scratch),
        compiler_params=pltpu.CompilerParams(vmem_limit_bytes=LIMIT),
        cost_estimate=pl.CostEstimate(flops=flops, bytes_accessed=size, transcendentals=0),
        name=name,
    )(*operands)


def product_kernel(chunks, away, other, tokens_ref, weight_ref, *rest):
    place = lax.axis_index("tensor")
    chip, core = place // 2, lax.rem(place, 2)
    parity = 1 - core if away else core
    columns = rest[-1].shape[-1]
    outs = rest[1:] if other else rest
    block = outs[0].shape[1]
    slots = [(out, k) for out in outs for k in range(out.shape[0])]
    for i, chunk in enumerate(chunks):
        group = 2 * lax.rem(chip + chunk, weight_ref.shape[1] // (2 * columns)) + parity
        weight = weight_ref[:, pl.ds(pl.multiple_of(group * columns, columns), columns)]
        product = jnp.dot(tokens_ref[...], weight, preferred_element_type=F32)
        if other:
            product += rest[0][i].astype(F32)
        product = product.astype(BF16)
        for first in range(0, product.shape[0], block):
            out, k = slots.pop(0)
            out[k] = product[first : first + block]


def products(chunks, away, tokens, weight, columns, outs, other=None):
    rows, features = tokens.shape
    return call(
        functools.partial(product_kernel, chunks, away, other is not None),
        [jax.ShapeDtypeStruct((*out, columns), BF16) for out in outs],
        (tokens, weight) + (() if other is None else (other,)),
        2 * rows * features * len(chunks) * columns,
        name="base",
    )


def combine_kernel(own_ref, up_ref, down_ref, *outs):
    rows = own_ref.shape[1]
    half = rows // 2
    up = up_ref[...].reshape(3 * half, -1)
    down = down_ref[...].reshape(3 * half, -1)
    own = own_ref[...].astype(F32)
    outs[0][...] = (own[0] + up[:rows].astype(F32)).astype(BF16)
    outs[1][:half] = (own[1, :half] + up[rows:].astype(F32)).astype(BF16)
    outs[1][half:] = own_ref[1, half:]
    outs[2][:half] = own_ref[2, :half]
    outs[2][half:] = (own[2, half:] + down[:half].astype(F32)).astype(BF16)
    outs[3][...] = (own[3] + down[half:].astype(F32)).astype(BF16)


def shift(array, by, groups):
    step = 2 * by
    return lax.ppermute(array, "tensor", [(i, (i + step) % groups) for i in range(groups)])


def sum_base(tokens, weight, columns, groups, after):
    rows = tokens.shape[0]
    half = rows // 2
    swap = [(i, i ^ 1) for i in range(groups)]
    far, near = (2, 4, 6), (0, 1, 3, 5, 7)
    (far_away,) = products(far, True, tokens, weight, columns, [(3, rows)])
    far_other = lax.ppermute(far_away, "tensor", swap)
    tokens, far_away = lax.optimization_barrier((tokens, far_away))
    (near_away,) = products(near, True, tokens, weight, columns, [(5, rows)])
    near_other = lax.ppermute(near_away, "tensor", swap)
    plus, minus = products(
        far, False, tokens, weight, columns, [(3, half), (3, half)], far_other
    )
    up, down = shift(plus, 1, groups), shift(minus, -1, groups)
    mine, own = products(near, False, tokens, weight, columns, [(1, rows), (4, rows)], near_other)
    sent = call(
        combine_kernel,
        [jax.ShapeDtypeStruct((rows, columns), BF16)] * 4,
        (own, up, down),
        rows * columns * 4,
        name="combine",
    )
    far_up, far_down = shift(sent[1], 3, groups), shift(sent[2], -3, groups)
    near_up, near_down = shift(sent[0], 1, groups), shift(sent[3], -1, groups)
    came = [far_up, far_down, near_up, near_down]
    after, *came = lax.optimization_barrier((after, *came))
    return after, [mine.reshape(rows, columns), *came]


def pack_kernel(labels_ref, tokens_ref, slots_ref, packed_ref):
    rows = tokens_ref.shape[0]
    labels = labels_ref[...]
    column = jnp.transpose(jnp.broadcast_to(labels, (8, rows)))[:, 0:1]
    earlier = lax.broadcasted_iota(jnp.int32, (rows, rows), 0) < lax.broadcasted_iota(
        jnp.int32, (rows, rows), 1
    )
    same = jnp.where((column == labels) & earlier, 1, 0)
    slots = labels * CAP + jnp.sum(same, axis=0, keepdims=True)
    slots_ref[...] = slots
    tokens = tokens_ref[...]
    block = 256

    @pl.loop(0, packed_ref.shape[0] // block)
    def _(i):
        first = pl.multiple_of(i * block, block)
        place = lax.broadcasted_iota(jnp.int32, (block, rows), 0) + first
        chosen = jnp.where(place == slots, 1.0, 0.0).astype(BF16)
        packed_ref[pl.ds(first, block), :] = jnp.dot(
            chosen, tokens, preferred_element_type=F32
        ).astype(BF16)


def pack(labels, tokens):
    rows, features = tokens.shape
    slots = ADAPTER_COUNT * CAP
    return call(
        pack_kernel,
        [
            jax.ShapeDtypeStruct((1, rows), jnp.int32),
            jax.ShapeDtypeStruct((slots, features), BF16),
        ],
        (labels, tokens),
        2 * slots * rows * features,
        name="pack",
    )


def down_kernel(rows_ref, weight_ref, out_ref):
    sources, slots, features = rows_ref.shape
    rank = weight_ref.shape[1]
    tile = QUAD * CAP
    owner = lax.broadcasted_iota(jnp.int32, (1, tile, 1), 1) // CAP
    for quad in range(slots // tile):
        rows = rows_ref[:, quad * tile : (quad + 1) * tile, :].reshape(sources * tile, features)
        weight = weight_ref[quad * QUAD : (quad + 1) * QUAD].reshape(QUAD * rank, features)
        product = lax.dot_general(
            rows, weight, (((1,), (1,)), ((), ())), preferred_element_type=F32
        ).reshape(sources, tile, QUAD * rank)
        lowered = jnp.zeros((sources, tile, rank), F32)
        for k in range(QUAD):
            lowered = jnp.where(owner == k, product[:, :, k * rank : (k + 1) * rank], lowered)
        lowered = lowered.reshape(sources // 2, 2, tile, rank)
        out_ref[:, quad * tile : (quad + 1) * tile, :] = jnp.concatenate(
            [lowered[:, 0], lowered[:, 1]], axis=-1
        ).astype(BF16)


def lower(received, weight):
    sources, slots, features = received.shape
    rank = weight.shape[1]
    return call(
        down_kernel,
        jax.ShapeDtypeStruct((sources // 2, slots, 2 * rank), BF16),
        (received, weight),
        2 * sources * slots * features * rank * QUAD,
        name="down",
    )


def up_kernel(lowered_ref, weight_ref, out_ref):
    pairs, slots, wide = lowered_ref.shape
    rank = wide // 2
    tile = QUAD * CAP
    columns = weight_ref.shape[2]
    shape = (pairs, tile, QUAD * rank)
    owner = lax.broadcasted_iota(jnp.int32, shape, 1) // CAP
    lane = lax.broadcasted_iota(jnp.int32, shape, 2) // rank
    own = (owner == lane).reshape(pairs * tile, QUAD * rank)
    for quad in range(slots // tile):
        both = lowered_ref[:, quad * tile : (quad + 1) * tile, :].reshape(pairs * tile, wide)
        weight = weight_ref[quad * QUAD : (quad + 1) * QUAD].reshape(QUAD * rank, columns)
        for half in range(2):
            lowered = both[:, half * rank : (half + 1) * rank]
            spread = jnp.where(own, jnp.concatenate([lowered] * QUAD, axis=-1), 0)
            out_ref[:, half, quad * tile : (quad + 1) * tile, :] = (
                jnp.dot(spread.astype(BF16), weight, preferred_element_type=F32)
                .astype(BF16)
                .reshape(pairs, tile, columns)
            )


def raise_rank(lowered, weight):
    pairs, slots, wide = lowered.shape
    columns = weight.shape[2]
    return call(
        up_kernel,
        jax.ShapeDtypeStruct((pairs, 2, slots, columns), BF16),
        (lowered, weight),
        pairs * 2 * slots * columns * wide * QUAD,
        name="up",
    )


def unpack_kernel(slots_ref, out_ref):
    rows, places = out_ref.shape
    slots = slots_ref[...]
    column = jnp.transpose(jnp.broadcast_to(slots, (8, rows)))[:, 0:1]
    block = 256
    for first in range(0, places, block):
        place = lax.broadcasted_iota(jnp.int32, (rows, block), 1) + first
        out_ref[:, first : first + block] = jnp.where(place == column, 1.0, 0.0).astype(BF16)


def finish_kernel(take_ref, returned_ref, accepted_ref, *rest):
    base_refs, (out_ref, chosen_ref) = rest[:-2], rest[-2:]
    rows = out_ref.shape[0]
    update = jnp.dot(take_ref[...], returned_ref[...], preferred_element_type=F32)
    base = base_refs[0][...].astype(F32)
    for base_ref in base_refs[1:]:
        base += base_ref[...].astype(F32)
    key_value = (base + update).astype(BF16)
    out_ref[...] = key_value
    count = chosen_ref.shape[0]
    place = lax.broadcasted_iota(jnp.int32, (count, rows), 1)
    column = jnp.transpose(jnp.broadcast_to(accepted_ref[...], (8, count)))[:, 0:1]
    take = jnp.where(place == column, 1.0, 0.0).astype(BF16)
    chosen_ref[...] = jnp.dot(take, key_value, preferred_element_type=F32).astype(BF16)


def cache_kernel(targets_ref, moved_ref, out_ref):
    count = targets_ref.shape[1]
    place = lax.broadcasted_iota(jnp.int32, (out_ref.shape[0], count), 0)
    take = jnp.where(place == targets_ref[...], 1.0, 0.0).astype(BF16)
    out_ref[...] = jnp.dot(take, moved_ref[...], preferred_element_type=F32).astype(BF16)


def exchange(array, axis, among=None):
    return lax.all_to_all(
        array, axis, split_axis=0, concat_axis=0, tiled=True, axis_index_groups=among
    )


def sum_over_tensor(partial, core, pairs, chips):
    both = lax.all_gather(partial, "tensor", axis=0, axis_index_groups=pairs)
    half = partial.shape[0] // 2
    mine = lax.dynamic_slice_in_dim(both, core * half, half, axis=1).astype(F32)
    mine = (mine[0] + mine[1]).astype(BF16)
    pieces = exchange(mine, "tensor", chips)
    pieces = pieces.reshape(half, 1, *partial.shape[1:])
    summed = jnp.sum(pieces.astype(F32), axis=0).astype(BF16)
    summed = jnp.broadcast_to(summed, (half, *partial.shape[1:]))
    mine = exchange(summed, "tensor", chips)
    return lax.all_gather(mine, "tensor", axis=0, axis_index_groups=pairs, tiled=True)


def per_device(
    tokens,
    row_adapter_index,
    adapter_down_weight,
    adapter_up_weight,
    key_value_weight,
    accepted_branch_rows,
    owner_cache_slots,
):
    owners, groups = lax.axis_size("adapter"), lax.axis_size("tensor")
    rows, features = tokens.shape
    columns = adapter_up_weight.shape[2]
    resident = adapter_down_weight.shape[0]
    here = resident * CAP

    core = lax.rem(lax.axis_index("tensor"), 2)
    pairs = [[2 * y, 2 * y + 1] for y in range(groups // 2)]
    chips = [[2 * y + c for y in range(groups // 2)] for c in range(2)]

    slots, packed = pack(row_adapter_index.reshape(1, rows), tokens)
    received = exchange(packed.reshape(owners, here, features), "adapter")

    tokens, slots = lax.optimization_barrier((tokens, slots))
    received, base = sum_base(tokens, key_value_weight, columns, groups, received)

    partial_rank = lower(received, jnp.swapaxes(adapter_down_weight, 1, 2))
    lowered = sum_over_tensor(partial_rank, core, pairs, chips)
    update = raise_rank(lowered, adapter_up_weight)
    returned = exchange(update.reshape(owners, here, columns), "adapter")
    take = call(
        unpack_kernel, jax.ShapeDtypeStruct((rows, owners * here), BF16), (slots,), 0, name="unpack"
    )
    accepted = accepted_branch_rows.reshape(1, -1)
    count = accepted.shape[1]
    key_value, chosen = call(
        finish_kernel,
        [
            jax.ShapeDtypeStruct((rows, columns), BF16),
            jax.ShapeDtypeStruct((count, columns), BF16),
        ],
        (take, returned.reshape(owners * here, columns), accepted, *base),
        2 * rows * owners * here * columns,
        name="finish",
    )
    moved = exchange(chosen.reshape(owners, -1, columns), "adapter").reshape(-1, columns)
    decode_cache = call(
        cache_kernel,
        jax.ShapeDtypeStruct((moved.shape[0], columns), BF16),
        (owner_cache_slots.reshape(1, -1), moved),
        2 * count * count * columns,
        name="cache",
    )
    return (key_value, decode_cache)


def solution(mesh):
    in_specs = (
        P("adapter", "tensor"),
        P("adapter", None),
        P("adapter", "tensor", None),
        P("adapter", None, "tensor"),
        P("tensor", None),
        P("adapter", None, None),
        P(None, "adapter", None),
    )
    out_specs = (P("adapter", "tensor"), P("adapter", "tensor"))
    return jax.shard_map(
        per_device, mesh=mesh, in_specs=in_specs, out_specs=out_specs, check_vma=False
    )
```

```python
import functools

import jax
import jax.numpy as jnp
from jax import lax
from jax.experimental import pallas as pl
from jax.experimental.pallas import tpu as pltpu
from jax.sharding import PartitionSpec as P

ADAPTER_COUNT = 512
CAP = 4
QUAD = 4
VMEM = pl.BlockSpec(memory_space=pltpu.VMEM)
HBM = pl.BlockSpec(memory_space=pltpu.HBM)
LIMIT = 20 * 1024 * 1024
WIDE = 60 * 1024 * 1024
BF16 = jnp.bfloat16
F32 = jnp.float32


def call(kernel, out_shape, operands, flops, scratch=(), name=None):
    outs = out_shape if isinstance(out_shape, (list, tuple)) else [out_shape]
    size = sum(x.size * x.dtype.itemsize for x in list(operands) + list(outs))
    return pl.pallas_call(
        kernel,
        out_shape=out_shape,
        in_specs=[VMEM] * len(operands),
        out_specs=jax.tree.map(lambda _: VMEM, out_shape),
        scratch_shapes=list(scratch),
        compiler_params=pltpu.CompilerParams(vmem_limit_bytes=LIMIT),
        cost_estimate=pl.CostEstimate(flops=flops, bytes_accessed=size, transcendentals=0),
        name=name,
    )(*operands)


def product_kernel(chunks, away, other, tokens_ref, weight_ref, *rest):
    place = lax.axis_index("tensor")
    chip, core = place // 2, lax.rem(place, 2)
    parity = 1 - core if away else core
    columns = rest[-1].shape[-1]
    outs = rest[1:] if other else rest
    block = outs[0].shape[1]
    slots = [(out, k) for out in outs for k in range(out.shape[0])]
    for i, chunk in enumerate(chunks):
        group = 2 * lax.rem(chip + chunk, weight_ref.shape[1] // (2 * columns)) + parity
        weight = weight_ref[:, pl.ds(pl.multiple_of(group * columns, columns), columns)]
        product = jnp.dot(tokens_ref[...], weight, preferred_element_type=F32)
        if other:
            product += rest[0][i].astype(F32)
        product = product.astype(BF16)
        for first in range(0, product.shape[0], block):
            out, k = slots.pop(0)
            out[k] = product[first : first + block]


def products(chunks, away, tokens, weight, columns, outs, other=None):
    rows, features = tokens.shape
    return call(
        functools.partial(product_kernel, chunks, away, other is not None),
        [jax.ShapeDtypeStruct((*out, columns), BF16) for out in outs],
        (tokens, weight) + (() if other is None else (other,)),
        2 * rows * features * len(chunks) * columns,
        name="base",
    )


def combine_kernel(own_ref, up_ref, down_ref, *outs):
    rows = own_ref.shape[1]
    half = rows // 2
    up = up_ref[...].reshape(3 * half, -1)
    down = down_ref[...].reshape(3 * half, -1)
    own = own_ref[...].astype(F32)
    outs[0][...] = (own[0] + up[:rows].astype(F32)).astype(BF16)
    outs[1][:half] = (own[1, :half] + up[rows:].astype(F32)).astype(BF16)
    outs[1][half:] = own_ref[1, half:]
    outs[2][:half] = own_ref[2, :half]
    outs[2][half:] = (own[2, half:] + down[:half].astype(F32)).astype(BF16)
    outs[3][...] = (own[3] + down[half:].astype(F32)).astype(BF16)


def shift(array, by, groups):
    step = 2 * by
    return lax.ppermute(array, "tensor", [(i, (i + step) % groups) for i in range(groups)])


def sum_base(tokens, weight, columns, groups, after):
    rows = tokens.shape[0]
    half = rows // 2
    swap = [(i, i ^ 1) for i in range(groups)]
    far, near = (2, 4, 6), (0, 1, 3, 5, 7)
    (far_away,) = products(far, True, tokens, weight, columns, [(3, rows)])
    far_other = lax.ppermute(far_away, "tensor", swap)
    tokens, far_away = lax.optimization_barrier((tokens, far_away))
    (near_away,) = products(near, True, tokens, weight, columns, [(5, rows)])
    near_other = lax.ppermute(near_away, "tensor", swap)
    plus, minus = products(
        far, False, tokens, weight, columns, [(3, half), (3, half)], far_other
    )
    up, down = shift(plus, 1, groups), shift(minus, -1, groups)
    mine, own = products(near, False, tokens, weight, columns, [(1, rows), (4, rows)], near_other)
    sent = call(
        combine_kernel,
        [jax.ShapeDtypeStruct((rows, columns), BF16)] * 4,
        (own, up, down),
        rows * columns * 4,
        name="combine",
    )
    far_up, far_down = shift(sent[1], 3, groups), shift(sent[2], -3, groups)
    near_up, near_down = shift(sent[0], 1, groups), shift(sent[3], -1, groups)
    after, far_up, far_down = lax.optimization_barrier((after, far_up, far_down))
    return after, [mine.reshape(rows, columns), far_up, far_down, near_up, near_down]


def pack_kernel(labels_hbm, tokens_hbm, slots_ref, packed_hbm, labels_ref, tokens_ref, parts, sems):
    rows = tokens_ref.shape[0]
    count, block = parts.shape[0], parts.shape[1]
    labels_in = pltpu.make_async_copy(labels_hbm, labels_ref, sems.at[count])
    tokens_in = pltpu.make_async_copy(tokens_hbm, tokens_ref, sems.at[count + 1])
    labels_in.start()
    tokens_in.start()
    labels_in.wait()
    labels = labels_ref[...]
    column = jnp.transpose(jnp.broadcast_to(labels, (8, rows)))[:, 0:1]
    earlier = lax.broadcasted_iota(jnp.int32, (rows, rows), 0) < lax.broadcasted_iota(
        jnp.int32, (rows, rows), 1
    )
    same = jnp.where((column == labels) & earlier, 1, 0)
    slots = labels * CAP + jnp.sum(same, axis=0, keepdims=True)
    slots_ref[...] = slots
    tokens_in.wait()
    tokens = tokens_ref[...]
    out = []
    for i in range(count):
        place = lax.broadcasted_iota(jnp.int32, (block, rows), 0) + i * block
        chosen = jnp.where(place == slots, 1.0, 0.0).astype(BF16)
        parts[i] = jnp.dot(chosen, tokens, preferred_element_type=F32).astype(BF16)
        out.append(
            pltpu.make_async_copy(
                parts.at[i], packed_hbm.at[pl.ds(i * block, block), :], sems.at[i]
            )
        )
        out[-1].start()
    for copy in out:
        copy.wait()


def pack(labels, tokens):
    rows, features = tokens.shape
    slots = ADAPTER_COUNT * CAP
    block = 256
    count = slots // block
    return pl.pallas_call(
        pack_kernel,
        out_shape=[
            jax.ShapeDtypeStruct((1, rows), jnp.int32),
            jax.ShapeDtypeStruct((slots, features), BF16),
        ],
        in_specs=[HBM, HBM],
        out_specs=[VMEM, HBM],
        scratch_shapes=[
            pltpu.VMEM((1, rows), jnp.int32),
            pltpu.VMEM((rows, features), BF16),
            pltpu.VMEM((count, block, features), BF16),
            pltpu.SemaphoreType.DMA((count + 2,)),
        ],
        compiler_params=pltpu.CompilerParams(vmem_limit_bytes=WIDE),
        cost_estimate=pl.CostEstimate(
            flops=2 * slots * rows * features,
            bytes_accessed=2 * (rows + slots) * features,
            transcendentals=0,
        ),
        name="pack",
    )(labels, tokens)


def down_kernel(rows_ref, weight_ref, out_ref):
    sources, tile, features = rows_ref.shape
    rank = weight_ref.shape[1]
    owner = lax.broadcasted_iota(jnp.int32, (1, tile, 1), 1) // CAP
    product = lax.dot_general(
        rows_ref[...].reshape(sources * tile, features),
        weight_ref[...].reshape(QUAD * rank, features),
        (((1,), (1,)), ((), ())),
        preferred_element_type=F32,
    ).reshape(sources, tile, QUAD * rank)
    lowered = jnp.zeros((sources, tile, rank), F32)
    for k in range(QUAD):
        lowered = jnp.where(owner == k, product[:, :, k * rank : (k + 1) * rank], lowered)
    lowered = lowered.reshape(sources // 2, 2, tile, rank)
    out_ref[...] = jnp.concatenate([lowered[:, 0], lowered[:, 1]], axis=-1).astype(BF16)


def lower(received, weight):
    sources, slots, features = received.shape
    rank = weight.shape[1]
    tile = QUAD * CAP
    return pl.pallas_call(
        down_kernel,
        grid=(slots // tile,),
        in_specs=[
            pl.BlockSpec((sources, tile, features), lambda i: (0, i, 0)),
            pl.BlockSpec((QUAD, rank, features), lambda i: (i, 0, 0)),
        ],
        out_specs=pl.BlockSpec((sources // 2, tile, 2 * rank), lambda i: (0, i, 0)),
        out_shape=jax.ShapeDtypeStruct((sources // 2, slots, 2 * rank), BF16),
        compiler_params=pltpu.CompilerParams(vmem_limit_bytes=WIDE),
        cost_estimate=pl.CostEstimate(
            flops=2 * sources * slots * features * rank * QUAD,
            bytes_accessed=2 * (sources * slots * features + slots // CAP * rank * features),
            transcendentals=0,
        ),
        name="down",
    )(received, weight)


def up_kernel(lowered_ref, weight_ref, out_ref):
    pairs, slots, wide = lowered_ref.shape
    rank = wide // 2
    tile = QUAD * CAP
    columns = weight_ref.shape[2]
    shape = (pairs, tile, QUAD * rank)
    owner = lax.broadcasted_iota(jnp.int32, shape, 1) // CAP
    lane = lax.broadcasted_iota(jnp.int32, shape, 2) // rank
    own = (owner == lane).reshape(pairs * tile, QUAD * rank)
    for quad in range(slots // tile):
        both = lowered_ref[:, quad * tile : (quad + 1) * tile, :].reshape(pairs * tile, wide)
        weight = weight_ref[quad * QUAD : (quad + 1) * QUAD].reshape(QUAD * rank, columns)
        for half in range(2):
            lowered = both[:, half * rank : (half + 1) * rank]
            spread = jnp.where(own, jnp.concatenate([lowered] * QUAD, axis=-1), 0)
            out_ref[:, half, quad * tile : (quad + 1) * tile, :] = (
                jnp.dot(spread.astype(BF16), weight, preferred_element_type=F32)
                .astype(BF16)
                .reshape(pairs, tile, columns)
            )


def raise_rank(lowered, weight):
    pairs, slots, wide = lowered.shape
    columns = weight.shape[2]
    return call(
        up_kernel,
        jax.ShapeDtypeStruct((pairs, 2, slots, columns), BF16),
        (lowered, weight),
        pairs * 2 * slots * columns * wide * QUAD,
        name="up",
    )


def finish_kernel(slots_ref, returned_ref, base_ref, accepted_ref, out_ref, chosen_ref):
    rows = out_ref.shape[0]
    places = returned_ref.shape[0]
    column = jnp.transpose(jnp.broadcast_to(slots_ref[...], (8, rows)))[:, 0:1]
    block = 256
    total = base_ref[...]
    for first in range(0, places, block):
        place = lax.broadcasted_iota(jnp.int32, (rows, block), 1) + first
        take = jnp.where(place == column, 1.0, 0.0).astype(BF16)
        total += jnp.dot(
            take, returned_ref[first : first + block], preferred_element_type=F32
        )
    key_value = total.astype(BF16)
    out_ref[...] = key_value
    count = chosen_ref.shape[0]
    place = lax.broadcasted_iota(jnp.int32, (count, rows), 1)
    column = jnp.transpose(jnp.broadcast_to(accepted_ref[...], (8, count)))[:, 0:1]
    take = jnp.where(place == column, 1.0, 0.0).astype(BF16)
    chosen_ref[...] = jnp.dot(take, key_value, preferred_element_type=F32).astype(BF16)


def cache_kernel(targets_ref, moved_ref, out_ref):
    count = targets_ref.shape[1]
    place = lax.broadcasted_iota(jnp.int32, (out_ref.shape[0], count), 0)
    take = jnp.where(place == targets_ref[...], 1.0, 0.0).astype(BF16)
    out_ref[...] = jnp.dot(take, moved_ref[...], preferred_element_type=F32).astype(BF16)


def exchange(array, axis, among=None):
    return lax.all_to_all(
        array, axis, split_axis=0, concat_axis=0, tiled=True, axis_index_groups=among
    )


def sum_over_tensor(partial, core, pairs, chips):
    both = lax.all_gather(partial, "tensor", axis=0, axis_index_groups=pairs)
    half = partial.shape[0] // 2
    mine = lax.dynamic_slice_in_dim(both, core * half, half, axis=1).astype(F32)
    mine = (mine[0] + mine[1]).astype(BF16)
    pieces = exchange(mine, "tensor", chips)
    pieces = pieces.reshape(half, 1, *partial.shape[1:])
    summed = jnp.sum(pieces.astype(F32), axis=0).astype(BF16)
    summed = jnp.broadcast_to(summed, (half, *partial.shape[1:]))
    mine = exchange(summed, "tensor", chips)
    return lax.all_gather(mine, "tensor", axis=0, axis_index_groups=pairs, tiled=True)


def per_device(
    tokens,
    row_adapter_index,
    adapter_down_weight,
    adapter_up_weight,
    key_value_weight,
    accepted_branch_rows,
    owner_cache_slots,
):
    owners, groups = lax.axis_size("adapter"), lax.axis_size("tensor")
    rows, features = tokens.shape
    columns = adapter_up_weight.shape[2]
    resident = adapter_down_weight.shape[0]
    here = resident * CAP

    core = lax.rem(lax.axis_index("tensor"), 2)
    pairs = [[2 * y, 2 * y + 1] for y in range(groups // 2)]
    chips = [[2 * y + c for y in range(groups // 2)] for c in range(2)]

    slots, packed = pack(row_adapter_index.reshape(1, rows), tokens)
    received = exchange(packed.reshape(owners, here, features), "adapter")

    tokens, slots = lax.optimization_barrier((tokens, slots))
    received, base = sum_base(tokens, key_value_weight, columns, groups, received)

    partial_rank = lower(received, jnp.swapaxes(adapter_down_weight, 1, 2))
    lowered = sum_over_tensor(partial_rank, core, pairs, chips)
    update = raise_rank(lowered, adapter_up_weight)
    returned = exchange(update.reshape(owners, here, columns), "adapter")
    base = sum(part.astype(F32) for part in base)
    accepted = accepted_branch_rows.reshape(1, -1)
    count = accepted.shape[1]
    key_value, chosen = call(
        finish_kernel,
        [
            jax.ShapeDtypeStruct((rows, columns), BF16),
            jax.ShapeDtypeStruct((count, columns), BF16),
        ],
        (slots, returned.reshape(owners * here, columns), base, accepted),
        2 * rows * owners * here * columns,
        name="finish",
    )
    moved = exchange(chosen.reshape(owners, -1, columns), "adapter").reshape(-1, columns)
    decode_cache = call(
        cache_kernel,
        jax.ShapeDtypeStruct((moved.shape[0], columns), BF16),
        (owner_cache_slots.reshape(1, -1), moved),
        2 * count * count * columns,
        name="cache",
    )
    return (key_value, decode_cache)


def solution(mesh):
    in_specs = (
        P("adapter", "tensor"),
        P("adapter", None),
        P("adapter", "tensor", None),
        P("adapter", None, "tensor"),
        P("tensor", None),
        P("adapter", None, None),
        P(None, "adapter", None),
    )
    out_specs = (P("adapter", "tensor"), P("adapter", "tensor"))
    return jax.shard_map(
        per_device, mesh=mesh, in_specs=in_specs, out_specs=out_specs, check_vma=False
    )
```

```python
import functools

import jax
import jax.numpy as jnp
from jax import lax
from jax.experimental import pallas as pl
from jax.experimental.pallas import tpu as pltpu
from jax.sharding import PartitionSpec as P

ADAPTER_COUNT = 512
CAP = 4
QUAD = 4
VMEM = pl.BlockSpec(memory_space=pltpu.VMEM)
HBM = pl.BlockSpec(memory_space=pltpu.HBM)
LIMIT = 16 * 1024 * 1024
WIDE = 60 * 1024 * 1024
BF16 = jnp.bfloat16
F32 = jnp.float32


def call(kernel, out_shape, operands, flops, scratch=(), name=None):
    outs = out_shape if isinstance(out_shape, (list, tuple)) else [out_shape]
    size = sum(x.size * x.dtype.itemsize for x in list(operands) + list(outs))
    return pl.pallas_call(
        kernel,
        out_shape=out_shape,
        in_specs=[VMEM] * len(operands),
        out_specs=jax.tree.map(lambda _: VMEM, out_shape),
        scratch_shapes=list(scratch),
        compiler_params=pltpu.CompilerParams(vmem_limit_bytes=LIMIT),
        cost_estimate=pl.CostEstimate(flops=flops, bytes_accessed=size, transcendentals=0),
        name=name,
    )(*operands)


def product_kernel(chunks, away, other, tokens_ref, weight_ref, *rest):
    place = lax.axis_index("tensor")
    chip, core = place // 2, lax.rem(place, 2)
    parity = 1 - core if away else core
    columns = rest[-1].shape[-1]
    outs = rest[1:] if other else rest
    block = outs[0].shape[1]
    slots = [(out, k) for out in outs for k in range(out.shape[0])]
    for i, chunk in enumerate(chunks):
        group = 2 * lax.rem(chip + chunk, weight_ref.shape[1] // (2 * columns)) + parity
        weight = weight_ref[:, pl.ds(pl.multiple_of(group * columns, columns), columns)]
        product = jnp.dot(tokens_ref[...], weight, preferred_element_type=F32)
        if other:
            product += rest[0][i].astype(F32)
        product = product.astype(BF16)
        for first in range(0, product.shape[0], block):
            out, k = slots.pop(0)
            out[k] = product[first : first + block]


def products(chunks, away, tokens, weight, columns, outs, other=None):
    rows, features = tokens.shape
    return call(
        functools.partial(product_kernel, chunks, away, other is not None),
        [jax.ShapeDtypeStruct((*out, columns), BF16) for out in outs],
        (tokens, weight) + (() if other is None else (other,)),
        2 * rows * features * len(chunks) * columns,
        name="base",
    )


def add(own, came):
    return (own.astype(F32) + came.astype(F32)).astype(BF16)


def shift(array, by, groups):
    step = 2 * by
    return lax.ppermute(array, "tensor", [(i, (i + step) % groups) for i in range(groups)])


def sum_base(tokens, weight, columns, groups, after):
    rows = tokens.shape[0]
    half = rows // 2
    swap = [(i, i ^ 1) for i in range(groups)]
    far, near = (4, 3, 5), (2, 6, 1, 7, 0)
    (far_away,) = products(far, True, tokens, weight, columns, [(3, rows)])
    far_other = lax.ppermute(far_away, "tensor", swap)
    tokens, far_away = lax.optimization_barrier((tokens, far_away))
    (near_away,) = products(near, True, tokens, weight, columns, [(5, rows)])
    near_other = lax.ppermute(near_away, "tensor", swap)
    outs = [(1, half)] * 2 + [(2, half)] * 2
    upper, lower_half, third, fifth = products(
        far, False, tokens, weight, columns, outs, far_other
    )
    up, down = shift(upper[0], 1, groups), shift(lower_half[0], -1, groups)
    outs = [(1, rows)] * 5
    second, sixth, first, seventh, mine = products(
        near, False, tokens, weight, columns, outs, near_other
    )
    third, fifth = call(
        ring_kernel,
        [jax.ShapeDtypeStruct((rows, columns), BF16)] * 2,
        (third, fifth, up, down),
        2 * rows * columns,
        name="ring",
    )
    up, down = shift(third, 1, groups), shift(fifth, -1, groups)
    up, down = shift(add(second[0], up), 1, groups), shift(add(sixth[0], down), -1, groups)
    after, up, down = lax.optimization_barrier((after, up, down))
    up, down = shift(add(first[0], up), 1, groups), shift(add(seventh[0], down), -1, groups)
    return after, [mine[0], up, down]


def ring_kernel(third_ref, fifth_ref, up_ref, down_ref, third_out, fifth_out):
    half = up_ref.shape[0]
    third_out[:half] = add(third_ref[0], up_ref[...])
    third_out[half:] = third_ref[1]
    fifth_out[:half] = fifth_ref[0]
    fifth_out[half:] = add(fifth_ref[1], down_ref[...])


def numbers(x):
    return x.astype(F32).astype(BF16)


def one_hot(mask):
    return jnp.where(mask, jnp.ones((), BF16), jnp.zeros((), BF16))


def pack_kernel(labels_hbm, tokens_hbm, slots_ref, packed_hbm, labels_ref, tokens_ref, parts, sems):
    rows = tokens_ref.shape[0]
    count, block = parts.shape[0], parts.shape[1]
    labels_in = pltpu.make_async_copy(labels_hbm, labels_ref, sems.at[count])
    tokens_in = pltpu.make_async_copy(tokens_hbm, tokens_ref, sems.at[count + 1])
    labels_in.start()
    tokens_in.start()
    labels_in.wait()
    labels = labels_ref[...]
    column = jnp.transpose(jnp.broadcast_to(labels, (8, rows)))[:, 0:1]
    step = 128
    earlier = lax.broadcasted_iota(jnp.int32, (step, step), 0) < lax.broadcasted_iota(
        jnp.int32, (step, step), 1
    )
    ranks = []
    for at in range(0, rows, step):
        here = labels[:, at : at + step]
        found = jnp.where((column[at : at + step] == here) & earlier, 1, 0)
        if at:
            before = jnp.where(column[:at] == here, 1, 0)
            found += jnp.sum(before.reshape(at // step, step, step), axis=0)
        ranks.append(jnp.sum(found, axis=0, keepdims=True))
    slots = labels * CAP + jnp.concatenate(ranks, axis=1)
    slots_ref[...] = slots
    tokens_in.wait()
    tokens = tokens_ref[...]
    place = numbers(lax.broadcasted_iota(jnp.int32, (block, rows), 0))
    out = []
    for i in range(count):
        chosen = one_hot(place == numbers(slots - i * block))
        parts[i] = jnp.dot(chosen, tokens, preferred_element_type=F32).astype(BF16)
        out.append(
            pltpu.make_async_copy(
                parts.at[i], packed_hbm.at[pl.ds(i * block, block), :], sems.at[i]
            )
        )
        out[-1].start()
    for copy in out:
        copy.wait()


def pack(labels, tokens):
    rows, features = tokens.shape
    slots = ADAPTER_COUNT * CAP
    block = 256
    count = slots // block
    return pl.pallas_call(
        pack_kernel,
        out_shape=[
            jax.ShapeDtypeStruct((1, rows), jnp.int32),
            jax.ShapeDtypeStruct((slots, features), BF16),
        ],
        in_specs=[HBM, HBM],
        out_specs=[VMEM, HBM],
        scratch_shapes=[
            pltpu.VMEM((1, rows), jnp.int32),
            pltpu.VMEM((rows, features), BF16),
            pltpu.VMEM((count, block, features), BF16),
            pltpu.SemaphoreType.DMA((count + 2,)),
        ],
        compiler_params=pltpu.CompilerParams(vmem_limit_bytes=WIDE),
        cost_estimate=pl.CostEstimate(
            flops=2 * slots * rows * features,
            bytes_accessed=2 * (rows + slots) * features,
            transcendentals=0,
        ),
        name="pack",
    )(labels, tokens)


def down_kernel(rows_hbm, weight_hbm, out_ref, rows_ref, weight_ref, sems):
    sources, slots, features = rows_ref.shape
    rank = weight_ref.shape[1]
    tile = QUAD * CAP
    quads, parts = slots // tile, 4
    share = sources // parts
    weights_in = [
        pltpu.make_async_copy(
            weight_hbm.at[pl.ds(q * QUAD, QUAD)], weight_ref.at[pl.ds(q * QUAD, QUAD)], sems.at[q]
        )
        for q in range(quads)
    ]
    rows_in = [
        pltpu.make_async_copy(
            rows_hbm.at[pl.ds(p * share, share)],
            rows_ref.at[pl.ds(p * share, share)],
            sems.at[quads + p],
        )
        for p in range(parts)
    ]
    for copy in weights_in[:1] + rows_in[:1] + weights_in[1:] + rows_in[1:]:
        copy.start()
    owner = lax.broadcasted_iota(jnp.int32, (1, tile, 1), 1) // CAP
    for p in range(parts):
        rows_in[p].wait()
        for q in range(quads):
            if p == 0:
                weights_in[q].wait()
            rows = rows_ref[p * share : (p + 1) * share, q * tile : (q + 1) * tile, :]
            product = lax.dot_general(
                rows.reshape(share * tile, features),
                weight_ref[q * QUAD : (q + 1) * QUAD].reshape(QUAD * rank, features),
                (((1,), (1,)), ((), ())),
                preferred_element_type=F32,
            ).reshape(share, tile, QUAD * rank)
            lowered = jnp.zeros((share, tile, rank), F32)
            for k in range(QUAD):
                lowered = jnp.where(owner == k, product[:, :, k * rank : (k + 1) * rank], lowered)
            lowered = lowered.reshape(share // 2, 2, tile, rank)
            out_ref[p * share // 2 : (p + 1) * share // 2, q * tile : (q + 1) * tile, :] = (
                jnp.concatenate([lowered[:, 0], lowered[:, 1]], axis=-1).astype(BF16)
            )


def lower(received, weight):
    sources, slots, features = received.shape
    rank = weight.shape[1]
    return pl.pallas_call(
        down_kernel,
        in_specs=[HBM, HBM],
        out_specs=VMEM,
        out_shape=jax.ShapeDtypeStruct((sources // 2, slots, 2 * rank), BF16),
        scratch_shapes=[
            pltpu.VMEM(received.shape, BF16),
            pltpu.VMEM(weight.shape, BF16),
            pltpu.SemaphoreType.DMA((slots // (QUAD * CAP) + 4,)),
        ],
        compiler_params=pltpu.CompilerParams(vmem_limit_bytes=WIDE),
        cost_estimate=pl.CostEstimate(
            flops=2 * sources * slots * features * rank * QUAD,
            bytes_accessed=2 * (sources * slots * features + slots // CAP * rank * features),
            transcendentals=0,
        ),
        name="down",
    )(received, weight)


def up_kernel(lowered_ref, weight_ref, out_ref):
    pairs, slots, wide = lowered_ref.shape
    rank = wide // 2
    tile = QUAD * CAP
    columns = weight_ref.shape[2]
    shape = (pairs, tile, QUAD * rank)
    owner = lax.broadcasted_iota(jnp.int32, shape, 1) // CAP
    lane = lax.broadcasted_iota(jnp.int32, shape, 2) // rank
    own = (owner == lane).reshape(pairs * tile, QUAD * rank)
    for quad in range(slots // tile):
        both = lowered_ref[:, quad * tile : (quad + 1) * tile, :].reshape(pairs * tile, wide)
        weight = weight_ref[quad * QUAD : (quad + 1) * QUAD].reshape(QUAD * rank, columns)
        for half in range(2):
            lowered = both[:, half * rank : (half + 1) * rank]
            spread = jnp.where(own, jnp.concatenate([lowered] * QUAD, axis=-1), 0)
            out_ref[:, half, quad * tile : (quad + 1) * tile, :] = (
                jnp.dot(spread.astype(BF16), weight, preferred_element_type=F32)
                .astype(BF16)
                .reshape(pairs, tile, columns)
            )


def raise_rank(lowered, weight):
    pairs, slots, wide = lowered.shape
    columns = weight.shape[2]
    return call(
        up_kernel,
        jax.ShapeDtypeStruct((pairs, 2, slots, columns), BF16),
        (lowered, weight),
        pairs * 2 * slots * columns * wide * QUAD,
        name="up",
    )


def finish_kernel(slots_ref, returned_ref, base_ref, accepted_ref, out_ref, chosen_ref):
    rows = out_ref.shape[0]
    places = returned_ref.shape[0]
    column = jnp.transpose(jnp.broadcast_to(slots_ref[...], (8, rows)))[:, 0:1]
    block = 256
    total = base_ref[...]
    place = numbers(lax.broadcasted_iota(jnp.int32, (rows, block), 1))
    for first in range(0, places, block):
        take = one_hot(place == numbers(column - first))
        total += jnp.dot(
            take, returned_ref[first : first + block], preferred_element_type=F32
        )
    key_value = total.astype(BF16)
    out_ref[...] = key_value
    count = chosen_ref.shape[0]
    place = lax.broadcasted_iota(jnp.int32, (count, rows), 1)
    column = jnp.transpose(jnp.broadcast_to(accepted_ref[...], (8, count)))[:, 0:1]
    take = jnp.where(place == column, 1.0, 0.0).astype(BF16)
    chosen_ref[...] = jnp.dot(take, key_value, preferred_element_type=F32).astype(BF16)


def cache_kernel(targets_ref, moved_ref, out_ref):
    count = targets_ref.shape[1]
    place = lax.broadcasted_iota(jnp.int32, (out_ref.shape[0], count), 0)
    take = jnp.where(place == targets_ref[...], 1.0, 0.0).astype(BF16)
    out_ref[...] = jnp.dot(take, moved_ref[...], preferred_element_type=F32).astype(BF16)


def exchange(array, axis, among=None):
    return lax.all_to_all(
        array, axis, split_axis=0, concat_axis=0, tiled=True, axis_index_groups=among
    )


def sum_over_tensor(partial, core, pairs, chips):
    both = lax.all_gather(partial, "tensor", axis=0, axis_index_groups=pairs)
    half = partial.shape[0] // 2
    mine = lax.dynamic_slice_in_dim(both, core * half, half, axis=1).astype(F32)
    mine = (mine[0] + mine[1]).astype(BF16)
    pieces = exchange(mine, "tensor", chips)
    pieces = pieces.reshape(half, 1, *partial.shape[1:])
    summed = jnp.sum(pieces.astype(F32), axis=0).astype(BF16)
    summed = jnp.broadcast_to(summed, (half, *partial.shape[1:]))
    mine = exchange(summed, "tensor", chips)
    return lax.all_gather(mine, "tensor", axis=0, axis_index_groups=pairs, tiled=True)


def per_device(
    tokens,
    row_adapter_index,
    adapter_down_weight,
    adapter_up_weight,
    key_value_weight,
    accepted_branch_rows,
    owner_cache_slots,
):
    owners, groups = lax.axis_size("adapter"), lax.axis_size("tensor")
    rows, features = tokens.shape
    columns = adapter_up_weight.shape[2]
    resident = adapter_down_weight.shape[0]
    here = resident * CAP

    core = lax.rem(lax.axis_index("tensor"), 2)
    pairs = [[2 * y, 2 * y + 1] for y in range(groups // 2)]
    chips = [[2 * y + c for y in range(groups // 2)] for c in range(2)]

    slots, packed = pack(row_adapter_index.reshape(1, rows), tokens)
    received = exchange(packed.reshape(owners, here, features), "adapter")

    tokens, slots = lax.optimization_barrier((tokens, slots))
    received, base = sum_base(tokens, key_value_weight, columns, groups, received)

    partial_rank = lower(received, jnp.swapaxes(adapter_down_weight, 1, 2))
    lowered = sum_over_tensor(partial_rank, core, pairs, chips)
    update = raise_rank(lowered, adapter_up_weight)
    returned = exchange(update.reshape(owners, here, columns), "adapter")
    base = sum(part.astype(F32) for part in base)
    accepted = accepted_branch_rows.reshape(1, -1)
    count = accepted.shape[1]
    key_value, chosen = call(
        finish_kernel,
        [
            jax.ShapeDtypeStruct((rows, columns), BF16),
            jax.ShapeDtypeStruct((count, columns), BF16),
        ],
        (slots, returned.reshape(owners * here, columns), base, accepted),
        2 * rows * owners * here * columns,
        name="finish",
    )
    moved = exchange(chosen.reshape(owners, -1, columns), "adapter").reshape(-1, columns)
    decode_cache = call(
        cache_kernel,
        jax.ShapeDtypeStruct((moved.shape[0], columns), BF16),
        (owner_cache_slots.reshape(1, -1), moved),
        2 * count * count * columns,
        name="cache",
    )
    return (key_value, decode_cache)


def solution(mesh):
    in_specs = (
        P("adapter", "tensor"),
        P("adapter", None),
        P("adapter", "tensor", None),
        P("adapter", None, "tensor"),
        P("tensor", None),
        P("adapter", None, None),
        P(None, "adapter", None),
    )
    out_specs = (P("adapter", "tensor"), P("adapter", "tensor"))
    return jax.shard_map(
        per_device, mesh=mesh, in_specs=in_specs, out_specs=out_specs, check_vma=False
    )
```

```python
import functools

import jax
import jax.numpy as jnp
from jax import lax
from jax.experimental import pallas as pl
from jax.experimental.pallas import tpu as pltpu
from jax.sharding import PartitionSpec as P

ADAPTER_COUNT = 512
CAP = 4
QUAD = 4
VMEM = pl.BlockSpec(memory_space=pltpu.VMEM)
HBM = pl.BlockSpec(memory_space=pltpu.HBM)
LIMIT = 16 * 1024 * 1024
WIDE = 60 * 1024 * 1024
BF16 = jnp.bfloat16
F32 = jnp.float32


def call(kernel, out_shape, operands, flops, scratch=(), name=None):
    outs = out_shape if isinstance(out_shape, (list, tuple)) else [out_shape]
    size = sum(x.size * x.dtype.itemsize for x in list(operands) + list(outs))
    return pl.pallas_call(
        kernel,
        out_shape=out_shape,
        in_specs=[VMEM] * len(operands),
        out_specs=jax.tree.map(lambda _: VMEM, out_shape),
        scratch_shapes=list(scratch),
        compiler_params=pltpu.CompilerParams(vmem_limit_bytes=LIMIT),
        cost_estimate=pl.CostEstimate(flops=flops, bytes_accessed=size, transcendentals=0),
        name=name,
    )(*operands)


def product_kernel(chunks, away, other, tokens_ref, weight_ref, *rest):
    place = lax.axis_index("tensor")
    chip, core = place // 2, lax.rem(place, 2)
    parity = 1 - core if away else core
    columns = rest[-1].shape[-1]
    outs = rest[1:] if other else rest
    block = outs[0].shape[1]
    slots = [(out, k) for out in outs for k in range(out.shape[0])]
    for i, chunk in enumerate(chunks):
        group = 2 * lax.rem(chip + chunk, weight_ref.shape[1] // (2 * columns)) + parity
        weight = weight_ref[:, pl.ds(pl.multiple_of(group * columns, columns), columns)]
        product = jnp.dot(tokens_ref[...], weight, preferred_element_type=F32)
        if other:
            product += rest[0][i].astype(F32)
        product = product.astype(BF16)
        for first in range(0, product.shape[0], block):
            out, k = slots.pop(0)
            out[k] = product[first : first + block]


def products(chunks, away, tokens, weight, columns, outs, other=None):
    rows, features = tokens.shape
    return call(
        functools.partial(product_kernel, chunks, away, other is not None),
        [jax.ShapeDtypeStruct((*out, columns), BF16) for out in outs],
        (tokens, weight) + (() if other is None else (other,)),
        2 * rows * features * len(chunks) * columns,
        name="base",
    )


def add(own, came):
    return (own.astype(F32) + came.astype(F32)).astype(BF16)


def shift(array, by, groups):
    step = 2 * by
    return lax.ppermute(array, "tensor", [(i, (i + step) % groups) for i in range(groups)])


def sum_base(tokens, weight, columns, groups, after, down_weight):
    rows = tokens.shape[0]
    half = rows // 2
    swap = [(i, i ^ 1) for i in range(groups)]
    far, near = (4, 3, 5), (2, 6, 1, 7, 0)
    (far_away,) = products(far, True, tokens, weight, columns, [(3, rows)])
    far_other = lax.ppermute(far_away, "tensor", swap)
    tokens, far_away = lax.optimization_barrier((tokens, far_away))
    (near_away,) = products(near, True, tokens, weight, columns, [(5, rows)])
    near_other = lax.ppermute(near_away, "tensor", swap)
    outs = [(1, half)] * 2 + [(2, half)] * 2
    upper, lower_half, third, fifth = products(
        far, False, tokens, weight, columns, outs, far_other
    )
    up, down = shift(upper[0], 1, groups), shift(lower_half[0], -1, groups)
    outs = [(1, rows)] * 5
    second, sixth, first, seventh, mine = products(
        near, False, tokens, weight, columns, outs, near_other
    )
    third, fifth = call(
        ring_kernel,
        [jax.ShapeDtypeStruct((rows, columns), BF16)] * 2,
        (third, fifth, up, down),
        2 * rows * columns,
        name="ring",
    )
    up, down = shift(third, 1, groups), shift(fifth, -1, groups)
    up, down = shift(add(second[0], up), 1, groups), shift(add(sixth[0], down), -1, groups)
    down_weight, up, down = lax.optimization_barrier((down_weight, up, down))
    down_weight = turn(down_weight)
    after, down_weight = lax.optimization_barrier((after, down_weight))
    up, down = shift(add(first[0], up), 1, groups), shift(add(seventh[0], down), -1, groups)
    return after, down_weight, [mine[0], up, down]


def ring_kernel(third_ref, fifth_ref, up_ref, down_ref, third_out, fifth_out):
    half = up_ref.shape[0]
    third_out[:half] = add(third_ref[0], up_ref[...])
    third_out[half:] = third_ref[1]
    fifth_out[:half] = fifth_ref[0]
    fifth_out[half:] = add(fifth_ref[1], down_ref[...])


def numbers(x):
    return x.astype(F32).astype(BF16)


def one_hot(mask):
    return jnp.where(mask, jnp.ones((), BF16), jnp.zeros((), BF16))


def pack_kernel(labels_hbm, tokens_hbm, slots_ref, packed_hbm, labels_ref, tokens_ref, parts, sems):
    rows = tokens_ref.shape[0]
    count, block = parts.shape[0], parts.shape[1]
    labels_in = pltpu.make_async_copy(labels_hbm, labels_ref, sems.at[count])
    tokens_in = pltpu.make_async_copy(tokens_hbm, tokens_ref, sems.at[count + 1])
    labels_in.start()
    tokens_in.start()
    labels_in.wait()
    labels = labels_ref[...]
    column = jnp.transpose(jnp.broadcast_to(labels, (8, rows)))[:, 0:1]
    step = 128
    earlier = lax.broadcasted_iota(jnp.int32, (step, step), 0) < lax.broadcasted_iota(
        jnp.int32, (step, step), 1
    )
    ranks = []
    for at in range(0, rows, step):
        here = labels[:, at : at + step]
        found = jnp.where((column[at : at + step] == here) & earlier, 1, 0)
        if at:
            before = jnp.where(column[:at] == here, 1, 0)
            found += jnp.sum(before.reshape(at // step, step, step), axis=0)
        ranks.append(jnp.sum(found, axis=0, keepdims=True))
    slots = labels * CAP + jnp.concatenate(ranks, axis=1)
    slots_ref[...] = slots
    tokens_in.wait()
    tokens = tokens_ref[...]
    place = numbers(lax.broadcasted_iota(jnp.int32, (block, rows), 0))
    out = []
    for i in range(count):
        chosen = one_hot(place == numbers(slots - i * block))
        parts[i] = jnp.dot(chosen, tokens, preferred_element_type=F32).astype(BF16)
        out.append(
            pltpu.make_async_copy(
                parts.at[i], packed_hbm.at[pl.ds(i * block, block), :], sems.at[i]
            )
        )
        out[-1].start()
    for copy in out:
        copy.wait()


def pack(labels, tokens):
    rows, features = tokens.shape
    slots = ADAPTER_COUNT * CAP
    block = 256
    count = slots // block
    return pl.pallas_call(
        pack_kernel,
        out_shape=[
            jax.ShapeDtypeStruct((1, rows), jnp.int32),
            jax.ShapeDtypeStruct((slots, features), BF16),
        ],
        in_specs=[HBM, HBM],
        out_specs=[VMEM, HBM],
        scratch_shapes=[
            pltpu.VMEM((1, rows), jnp.int32),
            pltpu.VMEM((rows, features), BF16),
            pltpu.VMEM((count, block, features), BF16),
            pltpu.SemaphoreType.DMA((count + 2,)),
        ],
        compiler_params=pltpu.CompilerParams(vmem_limit_bytes=WIDE),
        cost_estimate=pl.CostEstimate(
            flops=2 * slots * rows * features,
            bytes_accessed=2 * (rows + slots) * features,
            transcendentals=0,
        ),
        name="pack",
    )(labels, tokens)


def turn_kernel(weight_ref, out_ref):
    for quad in range(out_ref.shape[0]):
        for k in range(QUAD):
            turned = jnp.transpose(weight_ref[quad * QUAD + k])
            rank = turned.shape[1]
            out_ref[quad, :, k * rank : (k + 1) * rank] = turned


def turn(weight):
    adapters, rank, features = weight.shape
    return call(
        turn_kernel,
        jax.ShapeDtypeStruct((adapters // QUAD, features, QUAD * rank), BF16),
        (weight,),
        0,
        name="turn",
    )


def down_kernel(rows_hbm, weight_ref, out_ref, rows_ref, sems):
    sources, slots, features = rows_ref.shape
    rank = weight_ref.shape[2] // QUAD
    tile = QUAD * CAP
    parts = sems.shape[0]
    share = sources // parts
    rows_in = [
        pltpu.make_async_copy(
            rows_hbm.at[pl.ds(p * share, share)], rows_ref.at[pl.ds(p * share, share)], sems.at[p]
        )
        for p in range(parts)
    ]
    for copy in rows_in:
        copy.start()
    owner = lax.broadcasted_iota(jnp.int32, (1, tile, 1), 1) // CAP
    for p in range(parts):
        rows_in[p].wait()
        for quad in range(slots // tile):
            rows = rows_ref[p * share : (p + 1) * share, quad * tile : (quad + 1) * tile, :]
            product = jnp.dot(
                rows.reshape(share * tile, features),
                weight_ref[quad],
                preferred_element_type=F32,
            ).reshape(share, tile, QUAD * rank)
            lowered = jnp.zeros((share, tile, rank), F32)
            for k in range(QUAD):
                lowered = jnp.where(owner == k, product[:, :, k * rank : (k + 1) * rank], lowered)
            lowered = lowered.reshape(share // 2, 2, tile, rank)
            out_ref[
                p * share // 2 : (p + 1) * share // 2, quad * tile : (quad + 1) * tile, :
            ] = jnp.concatenate([lowered[:, 0], lowered[:, 1]], axis=-1).astype(BF16)


def lower(received, weight):
    sources, slots, features = received.shape
    rank = weight.shape[2] // QUAD
    return pl.pallas_call(
        down_kernel,
        in_specs=[HBM, VMEM],
        out_specs=VMEM,
        out_shape=jax.ShapeDtypeStruct((sources // 2, slots, 2 * rank), BF16),
        scratch_shapes=[
            pltpu.VMEM(received.shape, BF16),
            pltpu.SemaphoreType.DMA((4,)),
        ],
        compiler_params=pltpu.CompilerParams(vmem_limit_bytes=LIMIT),
        cost_estimate=pl.CostEstimate(
            flops=2 * sources * slots * features * rank * QUAD,
            bytes_accessed=2 * (sources * slots * features + slots // CAP * rank * features),
            transcendentals=0,
        ),
        name="down",
    )(received, weight)


def up_kernel(lowered_ref, weight_ref, out_ref):
    pairs, slots, wide = lowered_ref.shape
    rank = wide // 2
    tile = QUAD * CAP
    columns = weight_ref.shape[2]
    shape = (pairs, tile, QUAD * rank)
    owner = lax.broadcasted_iota(jnp.int32, shape, 1) // CAP
    lane = lax.broadcasted_iota(jnp.int32, shape, 2) // rank
    own = (owner == lane).reshape(pairs * tile, QUAD * rank)
    for quad in range(slots // tile):
        both = lowered_ref[:, quad * tile : (quad + 1) * tile, :].reshape(pairs * tile, wide)
        weight = weight_ref[quad * QUAD : (quad + 1) * QUAD].reshape(QUAD * rank, columns)
        for half in range(2):
            lowered = both[:, half * rank : (half + 1) * rank]
            spread = jnp.where(own, jnp.concatenate([lowered] * QUAD, axis=-1), 0)
            out_ref[:, half, quad * tile : (quad + 1) * tile, :] = (
                jnp.dot(spread.astype(BF16), weight, preferred_element_type=F32)
                .astype(BF16)
                .reshape(pairs, tile, columns)
            )


def raise_rank(lowered, weight):
    pairs, slots, wide = lowered.shape
    columns = weight.shape[2]
    return call(
        up_kernel,
        jax.ShapeDtypeStruct((pairs, 2, slots, columns), BF16),
        (lowered, weight),
        pairs * 2 * slots * columns * wide * QUAD,
        name="up",
    )


def finish_kernel(slots_ref, returned_ref, base_ref, accepted_ref, out_ref, chosen_ref):
    rows = out_ref.shape[0]
    places = returned_ref.shape[0]
    column = jnp.transpose(jnp.broadcast_to(slots_ref[...], (8, rows)))[:, 0:1]
    block = 256
    total = base_ref[...]
    place = numbers(lax.broadcasted_iota(jnp.int32, (rows, block), 1))
    for first in range(0, places, block):
        take = one_hot(place == numbers(column - first))
        total += jnp.dot(
            take, returned_ref[first : first + block], preferred_element_type=F32
        )
    key_value = total.astype(BF16)
    out_ref[...] = key_value
    count = chosen_ref.shape[0]
    place = lax.broadcasted_iota(jnp.int32, (count, rows), 1)
    column = jnp.transpose(jnp.broadcast_to(accepted_ref[...], (8, count)))[:, 0:1]
    take = jnp.where(place == column, 1.0, 0.0).astype(BF16)
    chosen_ref[...] = jnp.dot(take, key_value, preferred_element_type=F32).astype(BF16)


def cache_kernel(targets_ref, moved_ref, out_ref):
    count = targets_ref.shape[1]
    place = lax.broadcasted_iota(jnp.int32, (out_ref.shape[0], count), 0)
    take = jnp.where(place == targets_ref[...], 1.0, 0.0).astype(BF16)
    out_ref[...] = jnp.dot(take, moved_ref[...], preferred_element_type=F32).astype(BF16)


def exchange(array, axis, among=None):
    return lax.all_to_all(
        array, axis, split_axis=0, concat_axis=0, tiled=True, axis_index_groups=among
    )


def sum_over_tensor(partial, core, pairs, chips):
    both = lax.all_gather(partial, "tensor", axis=0, axis_index_groups=pairs)
    half = partial.shape[0] // 2
    mine = lax.dynamic_slice_in_dim(both, core * half, half, axis=1).astype(F32)
    mine = (mine[0] + mine[1]).astype(BF16)
    pieces = exchange(mine, "tensor", chips)
    pieces = pieces.reshape(half, 1, *partial.shape[1:])
    summed = jnp.sum(pieces.astype(F32), axis=0).astype(BF16)
    summed = jnp.broadcast_to(summed, (half, *partial.shape[1:]))
    mine = exchange(summed, "tensor", chips)
    return lax.all_gather(mine, "tensor", axis=0, axis_index_groups=pairs, tiled=True)


def per_device(
    tokens,
    row_adapter_index,
    adapter_down_weight,
    adapter_up_weight,
    key_value_weight,
    accepted_branch_rows,
    owner_cache_slots,
):
    owners, groups = lax.axis_size("adapter"), lax.axis_size("tensor")
    rows, features = tokens.shape
    columns = adapter_up_weight.shape[2]
    resident = adapter_down_weight.shape[0]
    here = resident * CAP

    core = lax.rem(lax.axis_index("tensor"), 2)
    pairs = [[2 * y, 2 * y + 1] for y in range(groups // 2)]
    chips = [[2 * y + c for y in range(groups // 2)] for c in range(2)]

    slots, packed = pack(row_adapter_index.reshape(1, rows), tokens)
    received = exchange(packed.reshape(owners, here, features), "adapter")

    tokens, slots = lax.optimization_barrier((tokens, slots))
    received, down_weight, base = sum_base(
        tokens,
        key_value_weight,
        columns,
        groups,
        received,
        jnp.swapaxes(adapter_down_weight, 1, 2),
    )

    partial_rank = lower(received, down_weight)
    lowered = sum_over_tensor(partial_rank, core, pairs, chips)
    update = raise_rank(lowered, adapter_up_weight)
    returned = exchange(update.reshape(owners, here, columns), "adapter")
    base = sum(part.astype(F32) for part in base)
    accepted = accepted_branch_rows.reshape(1, -1)
    count = accepted.shape[1]
    key_value, chosen = call(
        finish_kernel,
        [
            jax.ShapeDtypeStruct((rows, columns), BF16),
            jax.ShapeDtypeStruct((count, columns), BF16),
        ],
        (slots, returned.reshape(owners * here, columns), base, accepted),
        2 * rows * owners * here * columns,
        name="finish",
    )
    moved = exchange(chosen.reshape(owners, -1, columns), "adapter").reshape(-1, columns)
    decode_cache = call(
        cache_kernel,
        jax.ShapeDtypeStruct((moved.shape[0], columns), BF16),
        (owner_cache_slots.reshape(1, -1), moved),
        2 * count * count * columns,
        name="cache",
    )
    return (key_value, decode_cache)


def solution(mesh):
    in_specs = (
        P("adapter", "tensor"),
        P("adapter", None),
        P("adapter", "tensor", None),
        P("adapter", None, "tensor"),
        P("tensor", None),
        P("adapter", None, None),
        P(None, "adapter", None),
    )
    out_specs = (P("adapter", "tensor"), P("adapter", "tensor"))
    return jax.shard_map(
        per_device, mesh=mesh, in_specs=in_specs, out_specs=out_specs, check_vma=False
    )
```

```python
import functools

import jax
import jax.numpy as jnp
from jax import lax
from jax.experimental import pallas as pl
from jax.experimental.pallas import tpu as pltpu
from jax.sharding import PartitionSpec as P

ADAPTER_COUNT = 512
CAP = 4
QUAD = 4
VMEM = pl.BlockSpec(memory_space=pltpu.VMEM)
HBM = pl.BlockSpec(memory_space=pltpu.HBM)
LIMIT = 16 * 1024 * 1024
WIDE = 60 * 1024 * 1024
BF16 = jnp.bfloat16
F32 = jnp.float32


def call(kernel, out_shape, operands, flops, scratch=(), name=None):
    outs = out_shape if isinstance(out_shape, (list, tuple)) else [out_shape]
    size = sum(x.size * x.dtype.itemsize for x in list(operands) + list(outs))
    return pl.pallas_call(
        kernel,
        out_shape=out_shape,
        in_specs=[VMEM] * len(operands),
        out_specs=jax.tree.map(lambda _: VMEM, out_shape),
        scratch_shapes=list(scratch),
        compiler_params=pltpu.CompilerParams(vmem_limit_bytes=LIMIT),
        cost_estimate=pl.CostEstimate(flops=flops, bytes_accessed=size, transcendentals=0),
        name=name,
    )(*operands)


def product_kernel(chunks, away, other, tokens_ref, weight_ref, *rest):
    place = lax.axis_index("tensor")
    chip, core = place // 2, lax.rem(place, 2)
    parity = 1 - core if away else core
    columns = rest[-1].shape[-1]
    outs = rest[1:] if other else rest
    block = outs[0].shape[1]
    slots = [(out, k) for out in outs for k in range(out.shape[0])]
    for i, chunk in enumerate(chunks):
        group = 2 * lax.rem(chip + chunk, weight_ref.shape[1] // (2 * columns)) + parity
        weight = weight_ref[:, pl.ds(pl.multiple_of(group * columns, columns), columns)]
        product = jnp.dot(tokens_ref[...], weight, preferred_element_type=F32)
        if other:
            product += rest[0][i].astype(F32)
        product = product.astype(BF16)
        for first in range(0, product.shape[0], block):
            out, k = slots.pop(0)
            out[k] = product[first : first + block]


def products(chunks, away, tokens, weight, columns, outs, other=None):
    rows, features = tokens.shape
    return call(
        functools.partial(product_kernel, chunks, away, other is not None),
        [jax.ShapeDtypeStruct((*out, columns), BF16) for out in outs],
        (tokens, weight) + (() if other is None else (other,)),
        2 * rows * features * len(chunks) * columns,
        name="base",
    )


def add(own, came):
    return (own.astype(F32) + came.astype(F32)).astype(BF16)


def shift(array, by, groups):
    step = 2 * by
    return lax.ppermute(array, "tensor", [(i, (i + step) % groups) for i in range(groups)])


def sum_base(tokens, weight, columns, groups, after, down_weight):
    rows = tokens.shape[0]
    half = rows // 2
    swap = [(i, i ^ 1) for i in range(groups)]
    far, near = (4, 3, 5), (2, 6, 1, 7, 0)
    (far_away,) = products(far, True, tokens, weight, columns, [(3, rows)])
    far_other = lax.ppermute(far_away, "tensor", swap)
    tokens, far_away = lax.optimization_barrier((tokens, far_away))
    (near_away,) = products(near, True, tokens, weight, columns, [(5, rows)])
    near_other = lax.ppermute(near_away, "tensor", swap)
    outs = [(1, half)] * 2 + [(2, half)] * 2
    upper, lower_half, third, fifth = products(
        far, False, tokens, weight, columns, outs, far_other
    )
    up, down = shift(upper[0], 1, groups), shift(lower_half[0], -1, groups)
    outs = [(1, rows)] * 5
    second, sixth, first, seventh, mine = products(
        near, False, tokens, weight, columns, outs, near_other
    )
    third, fifth = call(
        ring_kernel,
        [jax.ShapeDtypeStruct((rows, columns), BF16)] * 2,
        (third, fifth, up, down),
        2 * rows * columns,
        name="ring",
    )
    up, down = shift(third, 1, groups), shift(fifth, -1, groups)
    up, down = shift(add(second[0], up), 1, groups), shift(add(sixth[0], down), -1, groups)
    down_weight, up, down = lax.optimization_barrier((down_weight, up, down))
    down_weight = turn(down_weight)
    after, down_weight = lax.optimization_barrier((after, down_weight))
    up, down = shift(add(first[0], up), 1, groups), shift(add(seventh[0], down), -1, groups)
    return after, down_weight, [mine[0], up, down]


def ring_kernel(third_ref, fifth_ref, up_ref, down_ref, third_out, fifth_out):
    half = up_ref.shape[0]
    third_out[:half] = add(third_ref[0], up_ref[...])
    third_out[half:] = third_ref[1]
    fifth_out[:half] = fifth_ref[0]
    fifth_out[half:] = add(fifth_ref[1], down_ref[...])


def numbers(x):
    return x.astype(F32).astype(BF16)


def one_hot(mask):
    return jnp.where(mask, jnp.ones((), BF16), jnp.zeros((), BF16))


def pack_kernel(labels_hbm, tokens_hbm, slots_ref, packed_hbm, labels_ref, tokens_ref, parts, sems):
    rows = tokens_ref.shape[0]
    count, block = parts.shape[0], parts.shape[1]
    labels_in = pltpu.make_async_copy(labels_hbm, labels_ref, sems.at[count])
    tokens_in = pltpu.make_async_copy(tokens_hbm, tokens_ref, sems.at[count + 1])
    labels_in.start()
    tokens_in.start()
    labels_in.wait()
    labels = labels_ref[...]
    column = jnp.transpose(jnp.broadcast_to(labels, (8, rows)))[:, 0:1]
    step = 128
    earlier = lax.broadcasted_iota(jnp.int32, (step, step), 0) < lax.broadcasted_iota(
        jnp.int32, (step, step), 1
    )
    ranks = []
    for at in range(0, rows, step):
        here = labels[:, at : at + step]
        found = jnp.where((column[at : at + step] == here) & earlier, 1, 0)
        if at:
            before = jnp.where(column[:at] == here, 1, 0)
            found += jnp.sum(before.reshape(at // step, step, step), axis=0)
        ranks.append(jnp.sum(found, axis=0, keepdims=True))
    slots = labels * CAP + jnp.concatenate(ranks, axis=1)
    slots_ref[...] = slots
    tokens_in.wait()
    tokens = tokens_ref[...]
    place = numbers(lax.broadcasted_iota(jnp.int32, (block // 2, rows), 0))
    out = []
    for i in range(count):
        chosen = jnp.concatenate(
            [one_hot(place == numbers(slots - at)) for at in (i * block, i * block + block // 2)]
        )
        parts[i] = jnp.dot(chosen, tokens, preferred_element_type=F32).astype(BF16)
        out.append(
            pltpu.make_async_copy(
                parts.at[i], packed_hbm.at[pl.ds(i * block, block), :], sems.at[i]
            )
        )
        out[-1].start()
    for copy in out:
        copy.wait()


def pack(labels, tokens):
    rows, features = tokens.shape
    slots = ADAPTER_COUNT * CAP
    block = 512
    count = slots // block
    return pl.pallas_call(
        pack_kernel,
        out_shape=[
            jax.ShapeDtypeStruct((1, rows), jnp.int32),
            jax.ShapeDtypeStruct((slots, features), BF16),
        ],
        in_specs=[HBM, HBM],
        out_specs=[VMEM, HBM],
        scratch_shapes=[
            pltpu.VMEM((1, rows), jnp.int32),
            pltpu.VMEM((rows, features), BF16),
            pltpu.VMEM((count, block, features), BF16),
            pltpu.SemaphoreType.DMA((count + 2,)),
        ],
        compiler_params=pltpu.CompilerParams(vmem_limit_bytes=WIDE),
        cost_estimate=pl.CostEstimate(
            flops=2 * slots * rows * features,
            bytes_accessed=2 * (rows + slots) * features,
            transcendentals=0,
        ),
        name="pack",
    )(labels, tokens)


def turn_kernel(weight_ref, out_ref):
    for quad in range(out_ref.shape[0]):
        for k in range(QUAD):
            turned = jnp.transpose(weight_ref[quad * QUAD + k])
            rank = turned.shape[1]
            out_ref[quad, :, k * rank : (k + 1) * rank] = turned


def turn(weight):
    adapters, rank, features = weight.shape
    return call(
        turn_kernel,
        jax.ShapeDtypeStruct((adapters // QUAD, features, QUAD * rank), BF16),
        (weight,),
        0,
        name="turn",
    )


def down_kernel(rows_hbm, weight_ref, out_ref, rows_ref, sems):
    quads, sources, tile, features = rows_ref.shape
    rank = weight_ref.shape[2] // QUAD
    rows_in = [
        pltpu.make_async_copy(
            rows_hbm.at[:, pl.ds(quad * tile, tile), :], rows_ref.at[quad], sems.at[quad]
        )
        for quad in range(quads)
    ]
    for copy in rows_in:
        copy.start()
    owner = lax.broadcasted_iota(jnp.int32, (1, tile, 1), 1) // CAP
    for quad in range(quads):
        rows_in[quad].wait()
        product = jnp.dot(
            rows_ref[quad].reshape(sources * tile, features),
            weight_ref[quad],
            preferred_element_type=F32,
        ).reshape(sources, tile, QUAD * rank)
        lowered = jnp.zeros((sources, tile, rank), F32)
        for k in range(QUAD):
            lowered = jnp.where(owner == k, product[:, :, k * rank : (k + 1) * rank], lowered)
        lowered = lowered.reshape(sources // 2, 2, tile, rank)
        out_ref[:, quad * tile : (quad + 1) * tile, :] = jnp.concatenate(
            [lowered[:, 0], lowered[:, 1]], axis=-1
        ).astype(BF16)


def lower(received, weight):
    sources, slots, features = received.shape
    rank = weight.shape[2] // QUAD
    tile = QUAD * CAP
    return pl.pallas_call(
        down_kernel,
        in_specs=[HBM, VMEM],
        out_specs=VMEM,
        out_shape=jax.ShapeDtypeStruct((sources // 2, slots, 2 * rank), BF16),
        scratch_shapes=[
            pltpu.VMEM((slots // tile, sources, tile, features), BF16),
            pltpu.SemaphoreType.DMA((slots // tile,)),
        ],
        compiler_params=pltpu.CompilerParams(vmem_limit_bytes=LIMIT),
        cost_estimate=pl.CostEstimate(
            flops=2 * sources * slots * features * rank * QUAD,
            bytes_accessed=2 * (sources * slots * features + slots // CAP * rank * features),
            transcendentals=0,
        ),
        name="down",
    )(received, weight)


def up_kernel(lowered_ref, weight_ref, out_ref):
    pairs, slots, wide = lowered_ref.shape
    rank = wide // 2
    tile = QUAD * CAP
    columns = weight_ref.shape[2]
    shape = (2 * pairs, tile, QUAD * rank)
    owner = lax.broadcasted_iota(jnp.int32, shape, 1) // CAP
    lane = lax.broadcasted_iota(jnp.int32, shape, 2) // rank
    own = (owner == lane).reshape(2 * pairs * tile, QUAD * rank)
    for quad in range(slots // tile):
        both = lowered_ref[:, quad * tile : (quad + 1) * tile, :].reshape(pairs * tile, wide)
        weight = weight_ref[quad * QUAD : (quad + 1) * QUAD].reshape(QUAD * rank, columns)
        lowered = jnp.concatenate([both[:, :rank], both[:, rank:]], axis=0)
        spread = jnp.where(own, jnp.concatenate([lowered] * QUAD, axis=-1), 0)
        update = jnp.dot(spread.astype(BF16), weight, preferred_element_type=F32).astype(BF16)
        update = update.reshape(2, pairs, tile, columns)
        for half in range(2):
            out_ref[:, half, quad * tile : (quad + 1) * tile, :] = update[half]


def raise_rank(lowered, weight):
    pairs, slots, wide = lowered.shape
    columns = weight.shape[2]
    return call(
        up_kernel,
        jax.ShapeDtypeStruct((pairs, 2, slots, columns), BF16),
        (lowered, weight),
        pairs * 2 * slots * columns * wide * QUAD,
        name="up",
    )


def finish_kernel(slots_ref, returned_ref, base_ref, accepted_ref, out_ref, chosen_ref):
    rows = out_ref.shape[0]
    places = returned_ref.shape[0]
    column = jnp.transpose(jnp.broadcast_to(slots_ref[...], (8, rows)))[:, 0:1]
    block = 256
    total = base_ref[...]
    place = numbers(lax.broadcasted_iota(jnp.int32, (rows, block), 1))
    for first in range(0, places, block):
        take = one_hot(place == numbers(column - first))
        total += jnp.dot(
            take, returned_ref[first : first + block], preferred_element_type=F32
        )
    key_value = total.astype(BF16)
    out_ref[...] = key_value
    count = chosen_ref.shape[0]
    place = lax.broadcasted_iota(jnp.int32, (count, rows), 1)
    column = jnp.transpose(jnp.broadcast_to(accepted_ref[...], (8, count)))[:, 0:1]
    take = jnp.where(place == column, 1.0, 0.0).astype(BF16)
    chosen_ref[...] = jnp.dot(take, key_value, preferred_element_type=F32).astype(BF16)


def cache_kernel(targets_ref, moved_ref, out_ref):
    count = targets_ref.shape[1]
    place = lax.broadcasted_iota(jnp.int32, (out_ref.shape[0], count), 0)
    take = jnp.where(place == targets_ref[...], 1.0, 0.0).astype(BF16)
    out_ref[...] = jnp.dot(take, moved_ref[...], preferred_element_type=F32).astype(BF16)


def exchange(array, axis, among=None):
    return lax.all_to_all(
        array, axis, split_axis=0, concat_axis=0, tiled=True, axis_index_groups=among
    )


def sum_over_tensor(partial, core, pairs, chips):
    both = lax.all_gather(partial, "tensor", axis=0, axis_index_groups=pairs)
    half = partial.shape[0] // 2
    mine = lax.dynamic_slice_in_dim(both, core * half, half, axis=1).astype(F32)
    mine = (mine[0] + mine[1]).astype(BF16)
    pieces = exchange(mine, "tensor", chips)
    pieces = pieces.reshape(half, 1, *partial.shape[1:])
    summed = jnp.sum(pieces.astype(F32), axis=0).astype(BF16)
    summed = jnp.broadcast_to(summed, (half, *partial.shape[1:]))
    mine = exchange(summed, "tensor", chips)
    return lax.all_gather(mine, "tensor", axis=0, axis_index_groups=pairs, tiled=True)


def per_device(
    tokens,
    row_adapter_index,
    adapter_down_weight,
    adapter_up_weight,
    key_value_weight,
    accepted_branch_rows,
    owner_cache_slots,
):
    owners, groups = lax.axis_size("adapter"), lax.axis_size("tensor")
    rows, features = tokens.shape
    columns = adapter_up_weight.shape[2]
    resident = adapter_down_weight.shape[0]
    here = resident * CAP

    core = lax.rem(lax.axis_index("tensor"), 2)
    pairs = [[2 * y, 2 * y + 1] for y in range(groups // 2)]
    chips = [[2 * y + c for y in range(groups // 2)] for c in range(2)]

    slots, packed = pack(row_adapter_index.reshape(1, rows), tokens)
    received = exchange(packed.reshape(owners, here, features), "adapter")

    tokens, slots = lax.optimization_barrier((tokens, slots))
    received, down_weight, base = sum_base(
        tokens,
        key_value_weight,
        columns,
        groups,
        received,
        jnp.swapaxes(adapter_down_weight, 1, 2),
    )

    partial_rank = lower(received, down_weight)
    lowered = sum_over_tensor(partial_rank, core, pairs, chips)
    update = raise_rank(lowered, adapter_up_weight)
    returned = exchange(update.reshape(owners, here, columns), "adapter")
    base = sum(part.astype(F32) for part in base)
    accepted = accepted_branch_rows.reshape(1, -1)
    count = accepted.shape[1]
    key_value, chosen = call(
        finish_kernel,
        [
            jax.ShapeDtypeStruct((rows, columns), BF16),
            jax.ShapeDtypeStruct((count, columns), BF16),
        ],
        (slots, returned.reshape(owners * here, columns), base, accepted),
        2 * rows * owners * here * columns,
        name="finish",
    )
    moved = exchange(chosen.reshape(owners, -1, columns), "adapter").reshape(-1, columns)
    decode_cache = call(
        cache_kernel,
        jax.ShapeDtypeStruct((moved.shape[0], columns), BF16),
        (owner_cache_slots.reshape(1, -1), moved),
        2 * count * count * columns,
        name="cache",
    )
    return (key_value, decode_cache)


def solution(mesh):
    in_specs = (
        P("adapter", "tensor"),
        P("adapter", None),
        P("adapter", "tensor", None),
        P("adapter", None, "tensor"),
        P("tensor", None),
        P("adapter", None, None),
        P(None, "adapter", None),
    )
    out_specs = (P("adapter", "tensor"), P("adapter", "tensor"))
    return jax.shard_map(
        per_device, mesh=mesh, in_specs=in_specs, out_specs=out_specs, check_vma=False
    )
```

```python
import functools

import jax
import jax.numpy as jnp
from jax import lax
from jax.experimental import pallas as pl
from jax.experimental.pallas import tpu as pltpu
from jax.sharding import PartitionSpec as P

ADAPTER_COUNT = 512
CAP = 4
QUAD = 4
VMEM = pl.BlockSpec(memory_space=pltpu.VMEM)
HBM = pl.BlockSpec(memory_space=pltpu.HBM)
LIMIT = 16 * 1024 * 1024
WIDE = 60 * 1024 * 1024
BF16 = jnp.bfloat16
F32 = jnp.float32


def call(kernel, out_shape, operands, flops, scratch=(), name=None):
    outs = out_shape if isinstance(out_shape, (list, tuple)) else [out_shape]
    size = sum(x.size * x.dtype.itemsize for x in list(operands) + list(outs))
    return pl.pallas_call(
        kernel,
        out_shape=out_shape,
        in_specs=[VMEM] * len(operands),
        out_specs=jax.tree.map(lambda _: VMEM, out_shape),
        scratch_shapes=list(scratch),
        compiler_params=pltpu.CompilerParams(vmem_limit_bytes=LIMIT),
        cost_estimate=pl.CostEstimate(flops=flops, bytes_accessed=size, transcendentals=0),
        name=name,
    )(*operands)


def product_kernel(chunks, away, other, tokens_ref, weight_ref, *rest):
    place = lax.axis_index("tensor")
    chip, core = place // 2, lax.rem(place, 2)
    parity = 1 - core if away else core
    columns = rest[-1].shape[-1]
    outs = rest[1:] if other else rest
    block = outs[0].shape[1]
    slots = [(out, k) for out in outs for k in range(out.shape[0])]
    for i, chunk in enumerate(chunks):
        group = 2 * lax.rem(chip + chunk, weight_ref.shape[1] // (2 * columns)) + parity
        weight = weight_ref[:, pl.ds(pl.multiple_of(group * columns, columns), columns)]
        product = jnp.dot(tokens_ref[...], weight, preferred_element_type=F32)
        if other:
            product += rest[0][i].astype(F32)
        product = product.astype(BF16)
        for first in range(0, product.shape[0], block):
            out, k = slots.pop(0)
            out[k] = product[first : first + block]


def products(chunks, away, tokens, weight, columns, outs, other=None):
    rows, features = tokens.shape
    return call(
        functools.partial(product_kernel, chunks, away, other is not None),
        [jax.ShapeDtypeStruct((*out, columns), BF16) for out in outs],
        (tokens, weight) + (() if other is None else (other,)),
        2 * rows * features * len(chunks) * columns,
        name="base",
    )


def add(own, came):
    return (own.astype(F32) + came.astype(F32)).astype(BF16)


def shift(array, by, groups):
    step = 2 * by
    return lax.ppermute(array, "tensor", [(i, (i + step) % groups) for i in range(groups)])


def sum_base(tokens, weight, columns, groups, after, down_weight):
    rows = tokens.shape[0]
    half = rows // 2
    swap = [(i, i ^ 1) for i in range(groups)]
    far, near = (4, 3, 5), (2, 6, 1, 7, 0)
    (far_away,) = products(far, True, tokens, weight, columns, [(3, rows)])
    far_other = lax.ppermute(far_away, "tensor", swap)
    tokens, far_away = lax.optimization_barrier((tokens, far_away))
    (near_away,) = products(near, True, tokens, weight, columns, [(5, rows)])
    near_other = lax.ppermute(near_away, "tensor", swap)
    outs = [(1, half)] * 2 + [(2, half)] * 2
    upper, lower_half, third, fifth = products(
        far, False, tokens, weight, columns, outs, far_other
    )
    up, down = shift(upper[0], 1, groups), shift(lower_half[0], -1, groups)
    outs = [(1, rows)] * 5
    second, sixth, first, seventh, mine = products(
        near, False, tokens, weight, columns, outs, near_other
    )
    third, fifth = call(
        ring_kernel,
        [jax.ShapeDtypeStruct((rows, columns), BF16)] * 2,
        (third, fifth, up, down),
        2 * rows * columns,
        name="ring",
    )
    up, down = shift(third, 1, groups), shift(fifth, -1, groups)
    up, down = shift(add(second[0], up), 1, groups), shift(add(sixth[0], down), -1, groups)
    down_weight, up, down = lax.optimization_barrier((down_weight, up, down))
    down_weight = turn(down_weight)
    after, down_weight = lax.optimization_barrier((after, down_weight))
    up, down = shift(add(first[0], up), 1, groups), shift(add(seventh[0], down), -1, groups)
    return after, down_weight, [mine[0], up, down]


def ring_kernel(third_ref, fifth_ref, up_ref, down_ref, third_out, fifth_out):
    half = up_ref.shape[0]
    third_out[:half] = add(third_ref[0], up_ref[...])
    third_out[half:] = third_ref[1]
    fifth_out[:half] = fifth_ref[0]
    fifth_out[half:] = add(fifth_ref[1], down_ref[...])


def numbers(x):
    return x.astype(F32).astype(BF16)


def one_hot(mask):
    return jnp.where(mask, jnp.ones((), BF16), jnp.zeros((), BF16))


def pack_kernel(labels_hbm, tokens_hbm, slots_ref, packed_hbm, labels_ref, tokens_ref, parts, sems):
    rows = tokens_ref.shape[0]
    count, block = parts.shape[0], parts.shape[1]
    labels_in = pltpu.make_async_copy(labels_hbm, labels_ref, sems.at[count])
    tokens_in = pltpu.make_async_copy(tokens_hbm, tokens_ref, sems.at[count + 1])
    labels_in.start()
    tokens_in.start()
    labels_in.wait()
    labels = labels_ref[...]
    column = jnp.transpose(jnp.broadcast_to(labels, (8, rows)))[:, 0:1]
    step = 128
    earlier = lax.broadcasted_iota(jnp.int32, (step, step), 0) < lax.broadcasted_iota(
        jnp.int32, (step, step), 1
    )
    ranks = []
    for at in range(0, rows, step):
        here = labels[:, at : at + step]
        found = jnp.where((column[at : at + step] == here) & earlier, 1, 0)
        if at:
            before = jnp.where(column[:at] == here, 1, 0)
            found += jnp.sum(before.reshape(at // step, step, step), axis=0)
        ranks.append(jnp.sum(found, axis=0, keepdims=True))
    slots = labels * CAP + jnp.concatenate(ranks, axis=1)
    slots_ref[...] = slots
    tokens_in.wait()
    place = numbers(lax.broadcasted_iota(jnp.int32, (block // 2, rows), 0))

    def copy_out(i):
        at = pl.multiple_of(i * block, block)
        return pltpu.make_async_copy(
            parts.at[i], packed_hbm.at[pl.ds(at, block), :], sems.at[i]
        )

    @pl.loop(0, count)
    def _(i):
        chosen = jnp.concatenate(
            [one_hot(place == numbers(slots - (i * block + at))) for at in (0, block // 2)]
        )
        parts[i] = jnp.dot(chosen, tokens_ref[...], preferred_element_type=F32).astype(BF16)
        copy_out(i).start()

    @pl.loop(0, count)
    def _(i):
        copy_out(i).wait()


def pack(labels, tokens):
    rows, features = tokens.shape
    slots = ADAPTER_COUNT * CAP
    block = 512
    count = slots // block
    return pl.pallas_call(
        pack_kernel,
        out_shape=[
            jax.ShapeDtypeStruct((1, rows), jnp.int32),
            jax.ShapeDtypeStruct((slots, features), BF16),
        ],
        in_specs=[HBM, HBM],
        out_specs=[VMEM, HBM],
        scratch_shapes=[
            pltpu.VMEM((1, rows), jnp.int32),
            pltpu.VMEM((rows, features), BF16),
            pltpu.VMEM((count, block, features), BF16),
            pltpu.SemaphoreType.DMA((count + 2,)),
        ],
        compiler_params=pltpu.CompilerParams(vmem_limit_bytes=WIDE),
        cost_estimate=pl.CostEstimate(
            flops=2 * slots * rows * features,
            bytes_accessed=2 * (rows + slots) * features,
            transcendentals=0,
        ),
        name="pack",
    )(labels, tokens)


def turn_kernel(weight_ref, out_ref):
    for quad in range(out_ref.shape[0]):
        for k in range(QUAD):
            turned = jnp.transpose(weight_ref[quad * QUAD + k])
            rank = turned.shape[1]
            out_ref[quad, :, k * rank : (k + 1) * rank] = turned


def turn(weight):
    adapters, rank, features = weight.shape
    return call(
        turn_kernel,
        jax.ShapeDtypeStruct((adapters // QUAD, features, QUAD * rank), BF16),
        (weight,),
        0,
        name="turn",
    )


def down_kernel(rows_hbm, weight_ref, out_ref, rows_ref, sems):
    quads, sources, tile, features = rows_ref.shape
    rank = weight_ref.shape[2] // QUAD
    rows_in = [
        pltpu.make_async_copy(
            rows_hbm.at[:, pl.ds(quad * tile, tile), :], rows_ref.at[quad], sems.at[quad]
        )
        for quad in range(quads)
    ]
    for copy in rows_in:
        copy.start()
    wide = QUAD * rank
    shape = (sources, tile, wide)
    owner = lax.broadcasted_iota(jnp.int32, shape, 1) // CAP
    own = owner == lax.broadcasted_iota(jnp.int32, shape, 2) // rank
    shape = (2 * wide, 2 * rank)
    line, lane = lax.broadcasted_iota(jnp.int32, shape, 0), lax.broadcasted_iota(jnp.int32, shape, 1)
    fold = jnp.where(line // wide * rank + line % rank == lane, 1.0, 0.0).astype(BF16)
    for quad in range(quads):
        rows_in[quad].wait()
        product = jnp.dot(
            rows_ref[quad].reshape(sources * tile, features),
            weight_ref[quad],
            preferred_element_type=F32,
        ).reshape(sources, tile, wide)
        lowered = jnp.where(own, product, 0.0).astype(BF16).reshape(sources // 2, 2, tile, wide)
        lowered = jnp.concatenate([lowered[:, 0], lowered[:, 1]], axis=-1)
        lowered = lowered.reshape(sources // 2 * tile, 2 * wide)
        out_ref[:, quad * tile : (quad + 1) * tile, :] = (
            jnp.dot(lowered, fold, preferred_element_type=F32)
            .astype(BF16)
            .reshape(sources // 2, tile, 2 * rank)
        )


def lower(received, weight):
    sources, slots, features = received.shape
    rank = weight.shape[2] // QUAD
    tile = QUAD * CAP
    return pl.pallas_call(
        down_kernel,
        in_specs=[HBM, VMEM],
        out_specs=VMEM,
        out_shape=jax.ShapeDtypeStruct((sources // 2, slots, 2 * rank), BF16),
        scratch_shapes=[
            pltpu.VMEM((slots // tile, sources, tile, features), BF16),
            pltpu.SemaphoreType.DMA((slots // tile,)),
        ],
        compiler_params=pltpu.CompilerParams(vmem_limit_bytes=LIMIT),
        cost_estimate=pl.CostEstimate(
            flops=2 * sources * slots * features * rank * QUAD,
            bytes_accessed=2 * (sources * slots * features + slots // CAP * rank * features),
            transcendentals=0,
        ),
        name="down",
    )(received, weight)


def up_kernel(lowered_ref, weight_ref, out_ref):
    pairs, slots, wide = lowered_ref.shape
    rank = wide // 2
    tile = QUAD * CAP
    columns = weight_ref.shape[2]
    shape = (2 * pairs, tile, QUAD * rank)
    owner = lax.broadcasted_iota(jnp.int32, shape, 1) // CAP
    lane = lax.broadcasted_iota(jnp.int32, shape, 2) // rank
    own = (owner == lane).reshape(2 * pairs * tile, QUAD * rank)
    for quad in range(slots // tile):
        both = lowered_ref[:, quad * tile : (quad + 1) * tile, :].reshape(pairs * tile, wide)
        weight = weight_ref[quad * QUAD : (quad + 1) * QUAD].reshape(QUAD * rank, columns)
        lowered = jnp.concatenate([both[:, :rank], both[:, rank:]], axis=0)
        spread = jnp.where(own, jnp.concatenate([lowered] * QUAD, axis=-1), 0)
        update = jnp.dot(spread.astype(BF16), weight, preferred_element_type=F32).astype(BF16)
        update = update.reshape(2, pairs, tile, columns)
        for half in range(2):
            out_ref[:, half, quad * tile : (quad + 1) * tile, :] = update[half]


def raise_rank(lowered, weight):
    pairs, slots, wide = lowered.shape
    columns = weight.shape[2]
    return call(
        up_kernel,
        jax.ShapeDtypeStruct((pairs, 2, slots, columns), BF16),
        (lowered, weight),
        pairs * 2 * slots * columns * wide * QUAD,
        name="up",
    )


def as_column(row):
    return jnp.transpose(jnp.broadcast_to(row, (8, row.shape[1])))[:, 0:1]


def prepare_kernel(slots_ref, accepted_ref, base_ref, take_ref, base_out):
    count, places = take_ref.shape
    rows = base_ref.shape[0]
    mine = lax.broadcasted_iota(jnp.int32, (count, rows), 1) == as_column(accepted_ref[...])
    slot = jnp.sum(jnp.where(mine, slots_ref[...], 0), axis=1, keepdims=True)
    place = lax.broadcasted_iota(jnp.int32, (count, places), 1)
    take_ref[...] = jnp.where(place == slot, 1.0, 0.0).astype(BF16)
    base_out[...] = jnp.dot(
        jnp.where(mine, 1.0, 0.0),
        base_ref[...],
        preferred_element_type=F32,
        precision=lax.Precision.HIGHEST,
    )


def choose_kernel(take_ref, returned_ref, base_ref, chosen_ref):
    update = jnp.dot(take_ref[...], returned_ref[...], preferred_element_type=F32)
    chosen_ref[...] = (base_ref[...] + update).astype(BF16)


def finish_kernel(slots_ref, returned_ref, base_ref, out_ref):
    rows = out_ref.shape[0]
    places = returned_ref.shape[0]
    column = as_column(slots_ref[...])
    block = 256
    total = base_ref[...]
    place = numbers(lax.broadcasted_iota(jnp.int32, (rows, block), 1))
    for first in range(0, places, block):
        take = one_hot(place == numbers(column - first))
        total += jnp.dot(
            take, returned_ref[first : first + block], preferred_element_type=F32
        )
    out_ref[...] = total.astype(BF16)


def cache_kernel(targets_ref, moved_ref, out_ref):
    count = targets_ref.shape[1]
    place = lax.broadcasted_iota(jnp.int32, (out_ref.shape[0], count), 0)
    take = jnp.where(place == targets_ref[...], 1.0, 0.0).astype(BF16)
    out_ref[...] = jnp.dot(take, moved_ref[...], preferred_element_type=F32).astype(BF16)


def exchange(array, axis, among=None):
    return lax.all_to_all(
        array, axis, split_axis=0, concat_axis=0, tiled=True, axis_index_groups=among
    )


def sum_over_tensor(partial, core, pairs, chips):
    both = lax.all_gather(partial, "tensor", axis=0, axis_index_groups=pairs)
    half = partial.shape[0] // 2
    mine = lax.dynamic_slice_in_dim(both, core * half, half, axis=1).astype(F32)
    mine = (mine[0] + mine[1]).astype(BF16)
    pieces = exchange(mine, "tensor", chips)
    pieces = pieces.reshape(half, 1, *partial.shape[1:])
    summed = jnp.sum(pieces.astype(F32), axis=0).astype(BF16)
    summed = jnp.broadcast_to(summed, (half, *partial.shape[1:]))
    mine = exchange(summed, "tensor", chips)
    return lax.all_gather(mine, "tensor", axis=0, axis_index_groups=pairs, tiled=True)


def per_device(
    tokens,
    row_adapter_index,
    adapter_down_weight,
    adapter_up_weight,
    key_value_weight,
    accepted_branch_rows,
    owner_cache_slots,
):
    owners, groups = lax.axis_size("adapter"), lax.axis_size("tensor")
    rows, features = tokens.shape
    columns = adapter_up_weight.shape[2]
    resident = adapter_down_weight.shape[0]
    here = resident * CAP

    core = lax.rem(lax.axis_index("tensor"), 2)
    pairs = [[2 * y, 2 * y + 1] for y in range(groups // 2)]
    chips = [[2 * y + c for y in range(groups // 2)] for c in range(2)]

    slots, packed = pack(row_adapter_index.reshape(1, rows), tokens)
    received = exchange(packed.reshape(owners, here, features), "adapter")

    tokens, slots = lax.optimization_barrier((tokens, slots))
    received, down_weight, base = sum_base(
        tokens,
        key_value_weight,
        columns,
        groups,
        received,
        jnp.swapaxes(adapter_down_weight, 1, 2),
    )

    partial_rank = lower(received, down_weight)
    lowered = sum_over_tensor(partial_rank, core, pairs, chips)
    update = raise_rank(lowered, adapter_up_weight)
    returned = exchange(update.reshape(owners, here, columns), "adapter")
    base = sum(part.astype(F32) for part in base)
    accepted = accepted_branch_rows.reshape(1, -1)
    count = accepted.shape[1]
    take, base_chosen = call(
        prepare_kernel,
        [
            jax.ShapeDtypeStruct((count, owners * here), BF16),
            jax.ShapeDtypeStruct((count, columns), F32),
        ],
        (slots, accepted, base),
        2 * count * rows * columns,
        name="prepare",
    )
    returned = returned.reshape(owners * here, columns)
    chosen = call(
        choose_kernel,
        jax.ShapeDtypeStruct((count, columns), BF16),
        (take, returned, base_chosen),
        2 * count * owners * here * columns,
        name="choose",
    )
    moved = exchange(chosen.reshape(owners, -1, columns), "adapter").reshape(-1, columns)
    returned, chosen = lax.optimization_barrier((returned, chosen))
    key_value = call(
        finish_kernel,
        jax.ShapeDtypeStruct((rows, columns), BF16),
        (slots, returned, base),
        2 * rows * owners * here * columns,
        name="finish",
    )
    decode_cache = call(
        cache_kernel,
        jax.ShapeDtypeStruct((moved.shape[0], columns), BF16),
        (owner_cache_slots.reshape(1, -1), moved),
        2 * count * count * columns,
        name="cache",
    )
    return (key_value, decode_cache)


def solution(mesh):
    in_specs = (
        P("adapter", "tensor"),
        P("adapter", None),
        P("adapter", "tensor", None),
        P("adapter", None, "tensor"),
        P("tensor", None),
        P("adapter", None, None),
        P(None, "adapter", None),
    )
    out_specs = (P("adapter", "tensor"), P("adapter", "tensor"))
    return jax.shard_map(
        per_device, mesh=mesh, in_specs=in_specs, out_specs=out_specs, check_vma=False
    )
```

```python
import functools

import jax
import jax.numpy as jnp
from jax import lax
from jax.experimental import pallas as pl
from jax.experimental.pallas import tpu as pltpu
from jax.sharding import PartitionSpec as P

ADAPTER_COUNT = 512
CAP = 4
QUAD = 4
VMEM = pl.BlockSpec(memory_space=pltpu.VMEM)
HBM = pl.BlockSpec(memory_space=pltpu.HBM)
LIMIT = 16 * 1024 * 1024
WIDE = 60 * 1024 * 1024
BF16 = jnp.bfloat16
F32 = jnp.float32


def call(kernel, out_shape, operands, flops, scratch=(), name=None):
    outs = out_shape if isinstance(out_shape, (list, tuple)) else [out_shape]
    size = sum(x.size * x.dtype.itemsize for x in list(operands) + list(outs))
    return pl.pallas_call(
        kernel,
        out_shape=out_shape,
        in_specs=[VMEM] * len(operands),
        out_specs=jax.tree.map(lambda _: VMEM, out_shape),
        scratch_shapes=list(scratch),
        compiler_params=pltpu.CompilerParams(vmem_limit_bytes=LIMIT),
        cost_estimate=pl.CostEstimate(flops=flops, bytes_accessed=size, transcendentals=0),
        name=name,
    )(*operands)


def product_kernel(chunks, away, other, tokens_ref, weight_ref, *rest):
    place = lax.axis_index("tensor")
    chip, core = place // 2, lax.rem(place, 2)
    parity = 1 - core if away else core
    columns = rest[-1].shape[-1]
    outs = rest[1:] if other else rest
    block = outs[0].shape[1]
    slots = [(out, k) for out in outs for k in range(out.shape[0])]
    for i, chunk in enumerate(chunks):
        group = 2 * lax.rem(chip + chunk, weight_ref.shape[1] // (2 * columns)) + parity
        weight = weight_ref[:, pl.ds(pl.multiple_of(group * columns, columns), columns)]
        product = jnp.dot(tokens_ref[...], weight, preferred_element_type=F32)
        if other:
            product += rest[0][i].astype(F32)
        product = product.astype(BF16)
        for first in range(0, product.shape[0], block):
            out, k = slots.pop(0)
            out[k] = product[first : first + block]


def products(chunks, away, tokens, weight, columns, outs, other=None):
    rows, features = tokens.shape
    return call(
        functools.partial(product_kernel, chunks, away, other is not None),
        [jax.ShapeDtypeStruct((*out, columns), BF16) for out in outs],
        (tokens, weight) + (() if other is None else (other,)),
        2 * rows * features * len(chunks) * columns,
        name="base",
    )


def add(own, came):
    return (own.astype(F32) + came.astype(F32)).astype(BF16)


def shift(array, by, groups):
    step = 2 * by
    return lax.ppermute(array, "tensor", [(i, (i + step) % groups) for i in range(groups)])


def sum_base(tokens, weight, columns, groups, after, down_weight):
    rows = tokens.shape[0]
    half = rows // 2
    swap = [(i, i ^ 1) for i in range(groups)]
    far, near = (4, 3, 5), (2, 6, 1, 7, 0)
    (far_away,) = products(far, True, tokens, weight, columns, [(3, rows)])
    far_other = lax.ppermute(far_away, "tensor", swap)
    tokens, far_away = lax.optimization_barrier((tokens, far_away))
    (near_away,) = products(near, True, tokens, weight, columns, [(5, rows)])
    near_other = lax.ppermute(near_away, "tensor", swap)
    outs = [(1, half)] * 2 + [(2, half)] * 2
    upper, lower_half, third, fifth = products(
        far, False, tokens, weight, columns, outs, far_other
    )
    up, down = shift(upper[0], 1, groups), shift(lower_half[0], -1, groups)
    outs = [(1, rows)] * 5
    second, sixth, first, seventh, mine = products(
        near, False, tokens, weight, columns, outs, near_other
    )
    third, fifth = call(
        ring_kernel,
        [jax.ShapeDtypeStruct((rows, columns), BF16)] * 2,
        (third, fifth, up, down),
        2 * rows * columns,
        name="ring",
    )
    up, down = shift(third, 1, groups), shift(fifth, -1, groups)
    up, down = shift(add(second[0], up), 1, groups), shift(add(sixth[0], down), -1, groups)
    down_weight, up, down = lax.optimization_barrier((down_weight, up, down))
    down_weight = keep(down_weight)
    after, down_weight = lax.optimization_barrier((after, down_weight))
    up, down = shift(add(first[0], up), 1, groups), shift(add(seventh[0], down), -1, groups)
    return after, down_weight, [mine[0], up, down]


def ring_kernel(third_ref, fifth_ref, up_ref, down_ref, third_out, fifth_out):
    half = up_ref.shape[0]
    third_out[:half] = add(third_ref[0], up_ref[...])
    third_out[half:] = third_ref[1]
    fifth_out[:half] = fifth_ref[0]
    fifth_out[half:] = add(fifth_ref[1], down_ref[...])


def numbers(x):
    return x.astype(F32).astype(BF16)


def one_hot(mask):
    return jnp.where(mask, jnp.ones((), BF16), jnp.zeros((), BF16))


def pack_kernel(labels_hbm, tokens_hbm, slots_ref, packed_hbm, labels_ref, tokens_ref, parts, sems):
    rows = tokens_ref.shape[0]
    count, block = parts.shape[0], parts.shape[1]
    labels_in = pltpu.make_async_copy(labels_hbm, labels_ref, sems.at[count])
    tokens_in = pltpu.make_async_copy(tokens_hbm, tokens_ref, sems.at[count + 1])
    labels_in.start()
    tokens_in.start()
    labels_in.wait()
    labels = labels_ref[...]
    column = jnp.transpose(jnp.broadcast_to(labels, (8, rows)))[:, 0:1]
    step = 128
    earlier = lax.broadcasted_iota(jnp.int32, (step, step), 0) < lax.broadcasted_iota(
        jnp.int32, (step, step), 1
    )
    ranks = []
    for at in range(0, rows, step):
        here = labels[:, at : at + step]
        found = jnp.where((column[at : at + step] == here) & earlier, 1, 0)
        if at:
            before = jnp.where(column[:at] == here, 1, 0)
            found += jnp.sum(before.reshape(at // step, step, step), axis=0)
        ranks.append(jnp.sum(found, axis=0, keepdims=True))
    slots = labels * CAP + jnp.concatenate(ranks, axis=1)
    slots_ref[...] = slots
    tokens_in.wait()
    tokens = tokens_ref[...]
    place = numbers(lax.broadcasted_iota(jnp.int32, (block // 2, rows), 0))
    out = []
    for i in range(count):
        chosen = jnp.concatenate(
            [one_hot(place == numbers(slots - at)) for at in (i * block, i * block + block // 2)]
        )
        parts[i] = jnp.dot(chosen, tokens, preferred_element_type=F32).astype(BF16)
        out.append(
            pltpu.make_async_copy(
                parts.at[i], packed_hbm.at[pl.ds(i * block, block), :], sems.at[i]
            )
        )
        out[-1].start()
    for copy in out:
        copy.wait()


def pack(labels, tokens):
    rows, features = tokens.shape
    slots = ADAPTER_COUNT * CAP
    block = 512
    count = slots // block
    return pl.pallas_call(
        pack_kernel,
        out_shape=[
            jax.ShapeDtypeStruct((1, rows), jnp.int32),
            jax.ShapeDtypeStruct((slots, features), BF16),
        ],
        in_specs=[HBM, HBM],
        out_specs=[VMEM, HBM],
        scratch_shapes=[
            pltpu.VMEM((1, rows), jnp.int32),
            pltpu.VMEM((rows, features), BF16),
            pltpu.VMEM((count, block, features), BF16),
            pltpu.SemaphoreType.DMA((count + 2,)),
        ],
        compiler_params=pltpu.CompilerParams(vmem_limit_bytes=WIDE),
        cost_estimate=pl.CostEstimate(
            flops=2 * slots * rows * features,
            bytes_accessed=2 * (rows + slots) * features,
            transcendentals=0,
        ),
        name="pack",
    )(labels, tokens)


def keep_kernel(weight_ref, out_ref):
    out_ref[...] = weight_ref[...]


def keep(weight):
    shape = jax.ShapeDtypeStruct(weight.shape, weight.dtype)
    return call(keep_kernel, shape, (weight,), 0, name="keep")


def down_kernel(rows_hbm, weight_ref, out_ref, rows_ref, sems):
    quads, sources, tile, features = rows_ref.shape
    rank = weight_ref.shape[1]
    rows_in = [
        pltpu.make_async_copy(
            rows_hbm.at[:, pl.ds(quad * tile, tile), :], rows_ref.at[quad], sems.at[quad]
        )
        for quad in range(quads)
    ]
    for copy in rows_in:
        copy.start()
    owner = lax.broadcasted_iota(jnp.int32, (1, tile, 1), 1) // CAP
    for quad in range(quads):
        rows_in[quad].wait()
        product = lax.dot_general(
            rows_ref[quad].reshape(sources * tile, features),
            weight_ref[quad * QUAD : (quad + 1) * QUAD].reshape(QUAD * rank, features),
            (((1,), (1,)), ((), ())),
            preferred_element_type=F32,
        ).reshape(sources, tile, QUAD * rank)
        lowered = jnp.zeros((sources, tile, rank), F32)
        for k in range(QUAD):
            lowered = jnp.where(owner == k, product[:, :, k * rank : (k + 1) * rank], lowered)
        lowered = lowered.reshape(sources // 2, 2, tile, rank)
        out_ref[:, quad * tile : (quad + 1) * tile, :] = jnp.concatenate(
            [lowered[:, 0], lowered[:, 1]], axis=-1
        ).astype(BF16)


def lower(received, weight):
    sources, slots, features = received.shape
    rank = weight.shape[1]
    tile = QUAD * CAP
    return pl.pallas_call(
        down_kernel,
        in_specs=[HBM, VMEM],
        out_specs=VMEM,
        out_shape=jax.ShapeDtypeStruct((sources // 2, slots, 2 * rank), BF16),
        scratch_shapes=[
            pltpu.VMEM((slots // tile, sources, tile, features), BF16),
            pltpu.SemaphoreType.DMA((slots // tile,)),
        ],
        compiler_params=pltpu.CompilerParams(vmem_limit_bytes=LIMIT),
        cost_estimate=pl.CostEstimate(
            flops=2 * sources * slots * features * rank * QUAD,
            bytes_accessed=2 * (sources * slots * features + slots // CAP * rank * features),
            transcendentals=0,
        ),
        name="down",
    )(received, weight)


def up_kernel(lowered_ref, weight_ref, out_ref):
    pairs, slots, wide = lowered_ref.shape
    rank = wide // 2
    tile = QUAD * CAP
    columns = weight_ref.shape[2]
    shape = (2 * pairs, tile, QUAD * rank)
    owner = lax.broadcasted_iota(jnp.int32, shape, 1) // CAP
    lane = lax.broadcasted_iota(jnp.int32, shape, 2) // rank
    own = (owner == lane).reshape(2 * pairs * tile, QUAD * rank)
    for quad in range(slots // tile):
        both = lowered_ref[:, quad * tile : (quad + 1) * tile, :].reshape(pairs * tile, wide)
        weight = weight_ref[quad * QUAD : (quad + 1) * QUAD].reshape(QUAD * rank, columns)
        lowered = jnp.concatenate([both[:, :rank], both[:, rank:]], axis=0)
        spread = jnp.where(own, jnp.concatenate([lowered] * QUAD, axis=-1), 0)
        update = jnp.dot(spread.astype(BF16), weight, preferred_element_type=F32).astype(BF16)
        update = update.reshape(2, pairs, tile, columns)
        for half in range(2):
            out_ref[:, half, quad * tile : (quad + 1) * tile, :] = update[half]


def raise_rank(lowered, weight):
    pairs, slots, wide = lowered.shape
    columns = weight.shape[2]
    return call(
        up_kernel,
        jax.ShapeDtypeStruct((pairs, 2, slots, columns), BF16),
        (lowered, weight),
        pairs * 2 * slots * columns * wide * QUAD,
        name="up",
    )


def as_column(row):
    return jnp.transpose(jnp.broadcast_to(row, (8, row.shape[1])))[:, 0:1]


def prepare_kernel(slots_ref, accepted_ref, base_ref, take_ref, base_out):
    count, places = take_ref.shape
    rows = base_ref.shape[0]
    mine = lax.broadcasted_iota(jnp.int32, (count, rows), 1) == as_column(accepted_ref[...])
    slot = jnp.sum(jnp.where(mine, slots_ref[...], 0), axis=1, keepdims=True)
    place = lax.broadcasted_iota(jnp.int32, (count, places), 1)
    take_ref[...] = jnp.where(place == slot, 1.0, 0.0).astype(BF16)
    base_out[...] = jnp.dot(
        jnp.where(mine, 1.0, 0.0),
        base_ref[...],
        preferred_element_type=F32,
        precision=lax.Precision.HIGHEST,
    )


def choose_kernel(take_ref, returned_ref, base_ref, chosen_ref):
    update = jnp.dot(take_ref[...], returned_ref[...], preferred_element_type=F32)
    chosen_ref[...] = (base_ref[...] + update).astype(BF16)


def finish_kernel(slots_ref, returned_ref, base_ref, out_ref):
    rows = out_ref.shape[0]
    places = returned_ref.shape[0]
    column = as_column(slots_ref[...])
    block = 256
    total = base_ref[...]
    place = numbers(lax.broadcasted_iota(jnp.int32, (rows, block), 1))
    for first in range(0, places, block):
        take = one_hot(place == numbers(column - first))
        total += jnp.dot(
            take, returned_ref[first : first + block], preferred_element_type=F32
        )
    out_ref[...] = total.astype(BF16)


def cache_kernel(targets_ref, moved_ref, out_ref):
    count = targets_ref.shape[1]
    place = lax.broadcasted_iota(jnp.int32, (out_ref.shape[0], count), 0)
    take = jnp.where(place == targets_ref[...], 1.0, 0.0).astype(BF16)
    out_ref[...] = jnp.dot(take, moved_ref[...], preferred_element_type=F32).astype(BF16)


def exchange(array, axis, among=None):
    return lax.all_to_all(
        array, axis, split_axis=0, concat_axis=0, tiled=True, axis_index_groups=among
    )


def sum_over_tensor(partial, core, pairs, chips):
    both = lax.all_gather(partial, "tensor", axis=0, axis_index_groups=pairs)
    half = partial.shape[0] // 2
    mine = lax.dynamic_slice_in_dim(both, core * half, half, axis=1).astype(F32)
    mine = (mine[0] + mine[1]).astype(BF16)
    pieces = exchange(mine, "tensor", chips)
    pieces = pieces.reshape(half, 1, *partial.shape[1:])
    summed = jnp.sum(pieces.astype(F32), axis=0).astype(BF16)
    summed = jnp.broadcast_to(summed, (half, *partial.shape[1:]))
    mine = exchange(summed, "tensor", chips)
    return lax.all_gather(mine, "tensor", axis=0, axis_index_groups=pairs, tiled=True)


def per_device(
    tokens,
    row_adapter_index,
    adapter_down_weight,
    adapter_up_weight,
    key_value_weight,
    accepted_branch_rows,
    owner_cache_slots,
):
    owners, groups = lax.axis_size("adapter"), lax.axis_size("tensor")
    rows, features = tokens.shape
    columns = adapter_up_weight.shape[2]
    resident = adapter_down_weight.shape[0]
    here = resident * CAP

    core = lax.rem(lax.axis_index("tensor"), 2)
    pairs = [[2 * y, 2 * y + 1] for y in range(groups // 2)]
    chips = [[2 * y + c for y in range(groups // 2)] for c in range(2)]

    slots, packed = pack(row_adapter_index.reshape(1, rows), tokens)
    received = exchange(packed.reshape(owners, here, features), "adapter")

    tokens, slots = lax.optimization_barrier((tokens, slots))
    received, down_weight, base = sum_base(
        tokens,
        key_value_weight,
        columns,
        groups,
        received,
        jnp.swapaxes(adapter_down_weight, 1, 2),
    )

    partial_rank = lower(received, down_weight)
    lowered = sum_over_tensor(partial_rank, core, pairs, chips)
    update = raise_rank(lowered, adapter_up_weight)
    returned = exchange(update.reshape(owners, here, columns), "adapter")
    base = sum(part.astype(F32) for part in base)
    accepted = accepted_branch_rows.reshape(1, -1)
    count = accepted.shape[1]
    take, base_chosen = call(
        prepare_kernel,
        [
            jax.ShapeDtypeStruct((count, owners * here), BF16),
            jax.ShapeDtypeStruct((count, columns), F32),
        ],
        (slots, accepted, base),
        2 * count * rows * columns,
        name="prepare",
    )
    returned = returned.reshape(owners * here, columns)
    chosen = call(
        choose_kernel,
        jax.ShapeDtypeStruct((count, columns), BF16),
        (take, returned, base_chosen),
        2 * count * owners * here * columns,
        name="choose",
    )
    moved = exchange(chosen.reshape(owners, -1, columns), "adapter").reshape(-1, columns)
    returned, chosen = lax.optimization_barrier((returned, chosen))
    key_value = call(
        finish_kernel,
        jax.ShapeDtypeStruct((rows, columns), BF16),
        (slots, returned, base),
        2 * rows * owners * here * columns,
        name="finish",
    )
    decode_cache = call(
        cache_kernel,
        jax.ShapeDtypeStruct((moved.shape[0], columns), BF16),
        (owner_cache_slots.reshape(1, -1), moved),
        2 * count * count * columns,
        name="cache",
    )
    return (key_value, decode_cache)


def solution(mesh):
    in_specs = (
        P("adapter", "tensor"),
        P("adapter", None),
        P("adapter", "tensor", None),
        P("adapter", None, "tensor"),
        P("tensor", None),
        P("adapter", None, None),
        P(None, "adapter", None),
    )
    out_specs = (P("adapter", "tensor"), P("adapter", "tensor"))
    return jax.shard_map(
        per_device, mesh=mesh, in_specs=in_specs, out_specs=out_specs, check_vma=False
    )
```

```python
import functools

import jax
import jax.numpy as jnp
from jax import lax
from jax.experimental import pallas as pl
from jax.experimental.pallas import tpu as pltpu
from jax.sharding import PartitionSpec as P

ADAPTER_COUNT = 512
CAP = 4
QUAD = 4
VMEM = pl.BlockSpec(memory_space=pltpu.VMEM)
HBM = pl.BlockSpec(memory_space=pltpu.HBM)
LIMIT = 16 * 1024 * 1024
WIDE = 60 * 1024 * 1024
BF16 = jnp.bfloat16
F32 = jnp.float32


def call(kernel, out_shape, operands, flops, scratch=(), name=None):
    outs = out_shape if isinstance(out_shape, (list, tuple)) else [out_shape]
    size = sum(x.size * x.dtype.itemsize for x in list(operands) + list(outs))
    return pl.pallas_call(
        kernel,
        out_shape=out_shape,
        in_specs=[VMEM] * len(operands),
        out_specs=jax.tree.map(lambda _: VMEM, out_shape),
        scratch_shapes=list(scratch),
        compiler_params=pltpu.CompilerParams(vmem_limit_bytes=LIMIT),
        cost_estimate=pl.CostEstimate(flops=flops, bytes_accessed=size, transcendentals=0),
        name=name,
    )(*operands)


def product_kernel(chunks, away, other, tokens_ref, weight_ref, *rest):
    place = lax.axis_index("tensor")
    chip, core = place // 2, lax.rem(place, 2)
    parity = 1 - core if away else core
    columns = rest[-1].shape[-1]
    outs = rest[1:] if other else rest
    block = outs[0].shape[1]
    slots = [(out, k) for out in outs for k in range(out.shape[0])]
    for i, chunk in enumerate(chunks):
        group = 2 * lax.rem(chip + chunk, weight_ref.shape[1] // (2 * columns)) + parity
        weight = weight_ref[:, pl.ds(pl.multiple_of(group * columns, columns), columns)]
        product = jnp.dot(tokens_ref[...], weight, preferred_element_type=F32)
        if other:
            product += rest[0][i].astype(F32)
        product = product.astype(BF16)
        for first in range(0, product.shape[0], block):
            out, k = slots.pop(0)
            out[k] = product[first : first + block]


def products(chunks, away, tokens, weight, columns, outs, other=None):
    rows, features = tokens.shape
    return call(
        functools.partial(product_kernel, chunks, away, other is not None),
        [jax.ShapeDtypeStruct((*out, columns), BF16) for out in outs],
        (tokens, weight) + (() if other is None else (other,)),
        2 * rows * features * len(chunks) * columns,
        name="base",
    )


def add(own, came):
    return (own.astype(F32) + came.astype(F32)).astype(BF16)


def shift(array, by, groups):
    step = 2 * by
    return lax.ppermute(array, "tensor", [(i, (i + step) % groups) for i in range(groups)])


def sum_base(tokens, weight, columns, groups, after, down_weight):
    rows = tokens.shape[0]
    half = rows // 2
    swap = [(i, i ^ 1) for i in range(groups)]
    far, near = (4, 3, 5), (2, 6, 1, 7, 0)
    (far_away,) = products(far, True, tokens, weight, columns, [(3, rows)])
    far_other = lax.ppermute(far_away, "tensor", swap)
    tokens, far_away = lax.optimization_barrier((tokens, far_away))
    (near_away,) = products(near, True, tokens, weight, columns, [(5, rows)])
    near_other = lax.ppermute(near_away, "tensor", swap)
    outs = [(1, half)] * 2 + [(2, half)] * 2
    upper, lower_half, third, fifth = products(
        far, False, tokens, weight, columns, outs, far_other
    )
    up, down = shift(upper[0], 1, groups), shift(lower_half[0], -1, groups)
    outs = [(1, rows)] * 5
    second, sixth, first, seventh, mine = products(
        near, False, tokens, weight, columns, outs, near_other
    )
    third, fifth = call(
        ring_kernel,
        [jax.ShapeDtypeStruct((rows, columns), BF16)] * 2,
        (third, fifth, up, down),
        2 * rows * columns,
        name="ring",
    )
    up, down = shift(third, 1, groups), shift(fifth, -1, groups)
    up, down = shift(add(second[0], up), 1, groups), shift(add(sixth[0], down), -1, groups)
    down_weight, up, down = lax.optimization_barrier((down_weight, up, down))
    down_weight = keep(down_weight)
    after, down_weight = lax.optimization_barrier((after, down_weight))
    up, down = shift(add(first[0], up), 1, groups), shift(add(seventh[0], down), -1, groups)
    return after, down_weight, [mine[0], up, down]


def ring_kernel(third_ref, fifth_ref, up_ref, down_ref, third_out, fifth_out):
    half = up_ref.shape[0]
    third_out[:half] = add(third_ref[0], up_ref[...])
    third_out[half:] = third_ref[1]
    fifth_out[:half] = fifth_ref[0]
    fifth_out[half:] = add(fifth_ref[1], down_ref[...])


def numbers(x):
    return x.astype(F32).astype(BF16)


def one_hot(mask):
    return jnp.where(mask, jnp.ones((), BF16), jnp.zeros((), BF16))


def pack_kernel(labels_hbm, tokens_hbm, slots_ref, packed_hbm, labels_ref, tokens_ref, parts, sems):
    rows = tokens_ref.shape[0]
    count, block = parts.shape[0], parts.shape[1]
    labels_in = pltpu.make_async_copy(labels_hbm, labels_ref, sems.at[count])
    tokens_in = pltpu.make_async_copy(tokens_hbm, tokens_ref, sems.at[count + 1])
    labels_in.start()
    tokens_in.start()
    labels_in.wait()
    labels = labels_ref[...]
    column = jnp.transpose(jnp.broadcast_to(labels, (8, rows)))[:, 0:1]
    step = 128
    earlier = lax.broadcasted_iota(jnp.int32, (step, step), 0) < lax.broadcasted_iota(
        jnp.int32, (step, step), 1
    )
    ranks = []
    for at in range(0, rows, step):
        here = labels[:, at : at + step]
        found = jnp.where((column[at : at + step] == here) & earlier, 1, 0)
        if at:
            before = jnp.where(column[:at] == here, 1, 0)
            found += jnp.sum(before.reshape(at // step, step, step), axis=0)
        ranks.append(jnp.sum(found, axis=0, keepdims=True))
    slots = labels * CAP + jnp.concatenate(ranks, axis=1)
    slots_ref[...] = slots
    tokens_in.wait()
    tokens = tokens_ref[...]
    place = numbers(lax.broadcasted_iota(jnp.int32, (block // 2, rows), 0))
    out = []
    for i in range(count):
        chosen = jnp.concatenate(
            [one_hot(place == numbers(slots - at)) for at in (i * block, i * block + block // 2)]
        )
        parts[i] = jnp.dot(chosen, tokens, preferred_element_type=F32).astype(BF16)
        out.append(
            pltpu.make_async_copy(
                parts.at[i], packed_hbm.at[pl.ds(i * block, block), :], sems.at[i]
            )
        )
        out[-1].start()
    for copy in out:
        copy.wait()


def pack(labels, tokens):
    rows, features = tokens.shape
    slots = ADAPTER_COUNT * CAP
    block = 512
    count = slots // block
    return pl.pallas_call(
        pack_kernel,
        out_shape=[
            jax.ShapeDtypeStruct((1, rows), jnp.int32),
            jax.ShapeDtypeStruct((slots, features), BF16),
        ],
        in_specs=[HBM, HBM],
        out_specs=[VMEM, HBM],
        scratch_shapes=[
            pltpu.VMEM((1, rows), jnp.int32),
            pltpu.VMEM((rows, features), BF16),
            pltpu.VMEM((count, block, features), BF16),
            pltpu.SemaphoreType.DMA((count + 2,)),
        ],
        compiler_params=pltpu.CompilerParams(vmem_limit_bytes=WIDE),
        cost_estimate=pl.CostEstimate(
            flops=2 * slots * rows * features,
            bytes_accessed=2 * (rows + slots) * features,
            transcendentals=0,
        ),
        name="pack",
    )(labels, tokens)


def keep_kernel(weight_ref, out_ref):
    out_ref[...] = weight_ref[...]


def keep(weight):
    shape = jax.ShapeDtypeStruct(weight.shape, weight.dtype)
    return call(keep_kernel, shape, (weight,), 0, name="keep")


def down_kernel(rows_ref, weight_ref, out_ref):
    sources, slots, features = rows_ref.shape
    rank = weight_ref.shape[1]
    tile = QUAD * CAP
    owner = lax.broadcasted_iota(jnp.int32, (1, tile, 1), 1) // CAP
    for quad in range(slots // tile):
        rows = rows_ref[:, quad * tile : (quad + 1) * tile, :].reshape(sources * tile, features)
        weight = weight_ref[quad * QUAD : (quad + 1) * QUAD].reshape(QUAD * rank, features)
        product = lax.dot_general(
            rows, weight, (((1,), (1,)), ((), ())), preferred_element_type=F32
        ).reshape(sources, tile, QUAD * rank)
        lowered = jnp.zeros((sources, tile, rank), F32)
        for k in range(QUAD):
            lowered = jnp.where(owner == k, product[:, :, k * rank : (k + 1) * rank], lowered)
        lowered = lowered.reshape(sources // 2, 2, tile, rank)
        out_ref[:, quad * tile : (quad + 1) * tile, :] = jnp.concatenate(
            [lowered[:, 0], lowered[:, 1]], axis=-1
        ).astype(BF16)


def lower(received, weight):
    sources, slots, features = received.shape
    rank = weight.shape[1]
    return call(
        down_kernel,
        jax.ShapeDtypeStruct((sources // 2, slots, 2 * rank), BF16),
        (received, weight),
        2 * sources * slots * features * rank * QUAD,
        name="down",
    )


def up_kernel(lowered_ref, weight_ref, out_ref):
    pairs, slots, wide = lowered_ref.shape
    rank = wide // 2
    tile = QUAD * CAP
    columns = weight_ref.shape[2]
    shape = (2 * pairs, tile, QUAD * rank)
    owner = lax.broadcasted_iota(jnp.int32, shape, 1) // CAP
    lane = lax.broadcasted_iota(jnp.int32, shape, 2) // rank
    own = (owner == lane).reshape(2 * pairs * tile, QUAD * rank)
    for quad in range(slots // tile):
        both = lowered_ref[:, quad * tile : (quad + 1) * tile, :].reshape(pairs * tile, wide)
        weight = weight_ref[quad * QUAD : (quad + 1) * QUAD].reshape(QUAD * rank, columns)
        lowered = jnp.concatenate([both[:, :rank], both[:, rank:]], axis=0)
        spread = jnp.where(own, jnp.concatenate([lowered] * QUAD, axis=-1), 0)
        update = jnp.dot(spread.astype(BF16), weight, preferred_element_type=F32).astype(BF16)
        update = update.reshape(2, pairs, tile, columns)
        for half in range(2):
            out_ref[:, half, quad * tile : (quad + 1) * tile, :] = update[half]


def raise_rank(lowered, weight):
    pairs, slots, wide = lowered.shape
    columns = weight.shape[2]
    return call(
        up_kernel,
        jax.ShapeDtypeStruct((pairs, 2, slots, columns), BF16),
        (lowered, weight),
        pairs * 2 * slots * columns * wide * QUAD,
        name="up",
    )


def finish_kernel(slots_ref, returned_ref, base_ref, accepted_ref, out_ref, chosen_ref):
    rows = out_ref.shape[0]
    places = returned_ref.shape[0]
    column = jnp.transpose(jnp.broadcast_to(slots_ref[...], (8, rows)))[:, 0:1]
    block = 256
    total = base_ref[...]
    place = numbers(lax.broadcasted_iota(jnp.int32, (rows, block), 1))
    for first in range(0, places, block):
        take = one_hot(place == numbers(column - first))
        total += jnp.dot(
            take, returned_ref[first : first + block], preferred_element_type=F32
        )
    key_value = total.astype(BF16)
    out_ref[...] = key_value
    count = chosen_ref.shape[0]
    place = lax.broadcasted_iota(jnp.int32, (count, rows), 1)
    column = jnp.transpose(jnp.broadcast_to(accepted_ref[...], (8, count)))[:, 0:1]
    take = jnp.where(place == column, 1.0, 0.0).astype(BF16)
    chosen_ref[...] = jnp.dot(take, key_value, preferred_element_type=F32).astype(BF16)


def cache_kernel(targets_ref, moved_ref, out_ref):
    count = targets_ref.shape[1]
    place = lax.broadcasted_iota(jnp.int32, (out_ref.shape[0], count), 0)
    take = jnp.where(place == targets_ref[...], 1.0, 0.0).astype(BF16)
    out_ref[...] = jnp.dot(take, moved_ref[...], preferred_element_type=F32).astype(BF16)


def exchange(array, axis, among=None):
    return lax.all_to_all(
        array, axis, split_axis=0, concat_axis=0, tiled=True, axis_index_groups=among
    )


def sum_over_tensor(partial, core, pairs, chips):
    both = lax.all_gather(partial, "tensor", axis=0, axis_index_groups=pairs)
    half = partial.shape[0] // 2
    mine = lax.dynamic_slice_in_dim(both, core * half, half, axis=1).astype(F32)
    mine = (mine[0] + mine[1]).astype(BF16)
    pieces = exchange(mine, "tensor", chips)
    pieces = pieces.reshape(half, 1, *partial.shape[1:])
    summed = jnp.sum(pieces.astype(F32), axis=0).astype(BF16)
    summed = jnp.broadcast_to(summed, (half, *partial.shape[1:]))
    mine = exchange(summed, "tensor", chips)
    return lax.all_gather(mine, "tensor", axis=0, axis_index_groups=pairs, tiled=True)


def per_device(
    tokens,
    row_adapter_index,
    adapter_down_weight,
    adapter_up_weight,
    key_value_weight,
    accepted_branch_rows,
    owner_cache_slots,
):
    owners, groups = lax.axis_size("adapter"), lax.axis_size("tensor")
    rows, features = tokens.shape
    columns = adapter_up_weight.shape[2]
    resident = adapter_down_weight.shape[0]
    here = resident * CAP

    core = lax.rem(lax.axis_index("tensor"), 2)
    pairs = [[2 * y, 2 * y + 1] for y in range(groups // 2)]
    chips = [[2 * y + c for y in range(groups // 2)] for c in range(2)]

    slots, packed = pack(row_adapter_index.reshape(1, rows), tokens)
    received = exchange(packed.reshape(owners, here, features), "adapter")

    tokens, slots = lax.optimization_barrier((tokens, slots))
    received, down_weight, base = sum_base(
        tokens,
        key_value_weight,
        columns,
        groups,
        received,
        jnp.swapaxes(adapter_down_weight, 1, 2),
    )

    partial_rank = lower(received, down_weight)
    lowered = sum_over_tensor(partial_rank, core, pairs, chips)
    update = raise_rank(lowered, adapter_up_weight)
    returned = exchange(update.reshape(owners, here, columns), "adapter")
    base = sum(part.astype(F32) for part in base)
    accepted = accepted_branch_rows.reshape(1, -1)
    count = accepted.shape[1]
    key_value, chosen = call(
        finish_kernel,
        [
            jax.ShapeDtypeStruct((rows, columns), BF16),
            jax.ShapeDtypeStruct((count, columns), BF16),
        ],
        (slots, returned.reshape(owners * here, columns), base, accepted),
        2 * rows * owners * here * columns,
        name="finish",
    )
    moved = exchange(chosen.reshape(owners, -1, columns), "adapter").reshape(-1, columns)
    decode_cache = call(
        cache_kernel,
        jax.ShapeDtypeStruct((moved.shape[0], columns), BF16),
        (owner_cache_slots.reshape(1, -1), moved),
        2 * count * count * columns,
        name="cache",
    )
    return (key_value, decode_cache)


def solution(mesh):
    in_specs = (
        P("adapter", "tensor"),
        P("adapter", None),
        P("adapter", "tensor", None),
        P("adapter", None, "tensor"),
        P("tensor", None),
        P("adapter", None, None),
        P(None, "adapter", None),
    )
    out_specs = (P("adapter", "tensor"), P("adapter", "tensor"))
    return jax.shard_map(
        per_device, mesh=mesh, in_specs=in_specs, out_specs=out_specs, check_vma=False
    )
```

```python
import functools

import jax
import jax.numpy as jnp
from jax import lax
from jax.experimental import pallas as pl
from jax.experimental.pallas import tpu as pltpu
from jax.sharding import PartitionSpec as P

ADAPTER_COUNT = 512
CAP = 4
QUAD = 4
VMEM = pl.BlockSpec(memory_space=pltpu.VMEM)
HBM = pl.BlockSpec(memory_space=pltpu.HBM)
LIMIT = 16 * 1024 * 1024
WIDE = 60 * 1024 * 1024
BF16 = jnp.bfloat16
F32 = jnp.float32


def call(kernel, out_shape, operands, flops, scratch=(), name=None):
    outs = out_shape if isinstance(out_shape, (list, tuple)) else [out_shape]
    size = sum(x.size * x.dtype.itemsize for x in list(operands) + list(outs))
    return pl.pallas_call(
        kernel,
        out_shape=out_shape,
        in_specs=[VMEM] * len(operands),
        out_specs=jax.tree.map(lambda _: VMEM, out_shape),
        scratch_shapes=list(scratch),
        compiler_params=pltpu.CompilerParams(vmem_limit_bytes=LIMIT),
        cost_estimate=pl.CostEstimate(flops=flops, bytes_accessed=size, transcendentals=0),
        name=name,
    )(*operands)


def product_kernel(chunks, away, other, tokens_ref, weight_ref, *rest):
    place = lax.axis_index("tensor")
    chip, core = place // 2, lax.rem(place, 2)
    parity = 1 - core if away else core
    columns = rest[-1].shape[-1]
    outs = rest[1:] if other else rest
    block = outs[0].shape[1]
    slots = [(out, k) for out in outs for k in range(out.shape[0])]
    for i, chunk in enumerate(chunks):
        group = 2 * lax.rem(chip + chunk, weight_ref.shape[1] // (2 * columns)) + parity
        weight = weight_ref[:, pl.ds(pl.multiple_of(group * columns, columns), columns)]
        product = jnp.dot(tokens_ref[...], weight, preferred_element_type=F32)
        if other:
            product += rest[0][i].astype(F32)
        product = product.astype(BF16)
        for first in range(0, product.shape[0], block):
            out, k = slots.pop(0)
            out[k] = product[first : first + block]


def products(chunks, away, tokens, weight, columns, outs, other=None):
    rows, features = tokens.shape
    return call(
        functools.partial(product_kernel, chunks, away, other is not None),
        [jax.ShapeDtypeStruct((*out, columns), BF16) for out in outs],
        (tokens, weight) + (() if other is None else (other,)),
        2 * rows * features * len(chunks) * columns,
        name="base",
    )


def add(own, came):
    return (own.astype(F32) + came.astype(F32)).astype(BF16)


def shift(array, by, groups):
    step = 2 * by
    return lax.ppermute(array, "tensor", [(i, (i + step) % groups) for i in range(groups)])


def sum_base(tokens, weight, columns, groups, after, down_weight):
    rows = tokens.shape[0]
    half = rows // 2
    swap = [(i, i ^ 1) for i in range(groups)]
    far, near = (4, 3, 5), (2, 6, 1, 7, 0)
    (far_away,) = products(far, True, tokens, weight, columns, [(3, rows)])
    far_other = lax.ppermute(far_away, "tensor", swap)
    tokens, far_away = lax.optimization_barrier((tokens, far_away))
    (near_away,) = products(near, True, tokens, weight, columns, [(5, rows)])
    near_other = lax.ppermute(near_away, "tensor", swap)
    outs = [(1, half)] * 2 + [(2, half)] * 2
    upper, lower_half, third, fifth = products(
        far, False, tokens, weight, columns, outs, far_other
    )
    up, down = shift(upper[0], 1, groups), shift(lower_half[0], -1, groups)
    outs = [(1, rows)] * 5
    second, sixth, first, seventh, mine = products(
        near, False, tokens, weight, columns, outs, near_other
    )
    third, fifth = call(
        ring_kernel,
        [jax.ShapeDtypeStruct((rows, columns), BF16)] * 2,
        (third, fifth, up, down),
        2 * rows * columns,
        name="ring",
    )
    up, down = shift(third, 1, groups), shift(fifth, -1, groups)
    up, down = shift(add(second[0], up), 1, groups), shift(add(sixth[0], down), -1, groups)
    down_weight, up, down = lax.optimization_barrier((down_weight, up, down))
    down_weight = keep(down_weight)
    after, down_weight = lax.optimization_barrier((after, down_weight))
    up, down = shift(add(first[0], up), 1, groups), shift(add(seventh[0], down), -1, groups)
    return after, down_weight, [mine[0], up, down]


def ring_kernel(third_ref, fifth_ref, up_ref, down_ref, third_out, fifth_out):
    half = up_ref.shape[0]
    third_out[:half] = add(third_ref[0], up_ref[...])
    third_out[half:] = third_ref[1]
    fifth_out[:half] = fifth_ref[0]
    fifth_out[half:] = add(fifth_ref[1], down_ref[...])


def numbers(x):
    return x.astype(F32).astype(BF16)


def one_hot(mask):
    return jnp.where(mask, jnp.ones((), BF16), jnp.zeros((), BF16))


def pack_kernel(labels_hbm, tokens_hbm, slots_ref, packed_hbm, labels_ref, tokens_ref, parts, sems):
    rows = tokens_ref.shape[0]
    count, block = parts.shape[0], parts.shape[1]
    labels_in = pltpu.make_async_copy(labels_hbm, labels_ref, sems.at[count])
    tokens_in = pltpu.make_async_copy(tokens_hbm, tokens_ref, sems.at[count + 1])
    labels_in.start()
    tokens_in.start()
    labels_in.wait()
    labels = labels_ref[...]
    column = jnp.transpose(jnp.broadcast_to(labels, (8, rows)))[:, 0:1]
    step = 128
    earlier = lax.broadcasted_iota(jnp.int32, (step, step), 0) < lax.broadcasted_iota(
        jnp.int32, (step, step), 1
    )
    ranks = []
    for at in range(0, rows, step):
        here = labels[:, at : at + step]
        found = jnp.where((column[at : at + step] == here) & earlier, 1, 0)
        if at:
            before = jnp.where(column[:at] == here, 1, 0)
            found += jnp.sum(before.reshape(at // step, step, step), axis=0)
        ranks.append(jnp.sum(found, axis=0, keepdims=True))
    slots = labels * CAP + jnp.concatenate(ranks, axis=1)
    slots_ref[...] = slots
    tokens_in.wait()
    tokens = tokens_ref[...]
    place = numbers(lax.broadcasted_iota(jnp.int32, (block // 2, rows), 0))
    out = []
    for i in range(count):
        chosen = jnp.concatenate(
            [one_hot(place == numbers(slots - at)) for at in (i * block, i * block + block // 2)]
        )
        parts[i] = jnp.dot(chosen, tokens, preferred_element_type=F32).astype(BF16)
        out.append(
            pltpu.make_async_copy(
                parts.at[i], packed_hbm.at[pl.ds(i * block, block), :], sems.at[i]
            )
        )
        out[-1].start()
    for copy in out:
        copy.wait()


def pack(labels, tokens):
    rows, features = tokens.shape
    slots = ADAPTER_COUNT * CAP
    block = 512
    count = slots // block
    return pl.pallas_call(
        pack_kernel,
        out_shape=[
            jax.ShapeDtypeStruct((1, rows), jnp.int32),
            jax.ShapeDtypeStruct((slots, features), BF16),
        ],
        in_specs=[HBM, HBM],
        out_specs=[VMEM, HBM],
        scratch_shapes=[
            pltpu.VMEM((1, rows), jnp.int32),
            pltpu.VMEM((rows, features), BF16),
            pltpu.VMEM((count, block, features), BF16),
            pltpu.SemaphoreType.DMA((count + 2,)),
        ],
        compiler_params=pltpu.CompilerParams(vmem_limit_bytes=WIDE),
        cost_estimate=pl.CostEstimate(
            flops=2 * slots * rows * features,
            bytes_accessed=2 * (rows + slots) * features,
            transcendentals=0,
        ),
        name="pack",
    )(labels, tokens)


def keep_kernel(weight_ref, out_ref):
    out_ref[...] = weight_ref[...]


def keep(weight):
    shape = jax.ShapeDtypeStruct(weight.shape, weight.dtype)
    return call(keep_kernel, shape, (weight,), 0, name="keep")


def down_kernel(rows_ref, weight_ref, out_ref):
    sources, slots, features = rows_ref.shape
    rank = weight_ref.shape[1]
    tile = QUAD * CAP
    owner = lax.broadcasted_iota(jnp.int32, (1, tile, 1), 1) // CAP
    for quad in range(slots // tile):
        rows = rows_ref[:, quad * tile : (quad + 1) * tile, :].reshape(sources * tile, features)
        weight = weight_ref[quad * QUAD : (quad + 1) * QUAD].reshape(QUAD * rank, features)
        product = lax.dot_general(
            rows, weight, (((1,), (1,)), ((), ())), preferred_element_type=F32
        ).reshape(sources, tile, QUAD * rank)
        lowered = jnp.zeros((sources, tile, rank), F32)
        for k in range(QUAD):
            lowered = jnp.where(owner == k, product[:, :, k * rank : (k + 1) * rank], lowered)
        lowered = lowered.reshape(sources // 2, 2, tile, rank)
        out_ref[:, quad * tile : (quad + 1) * tile, :] = jnp.concatenate(
            [lowered[:, 0], lowered[:, 1]], axis=-1
        ).astype(BF16)


def lower(received, weight):
    sources, slots, features = received.shape
    rank = weight.shape[1]
    return call(
        down_kernel,
        jax.ShapeDtypeStruct((sources // 2, slots, 2 * rank), BF16),
        (received, weight),
        2 * sources * slots * features * rank * QUAD,
        name="down",
    )


def up_kernel(lowered_ref, weight_ref, out_ref):
    pairs, slots, wide = lowered_ref.shape
    rank = wide // 2
    tile = QUAD * CAP
    columns = weight_ref.shape[2]
    shape = (2 * pairs, tile, QUAD * rank)
    owner = lax.broadcasted_iota(jnp.int32, shape, 1) // CAP
    lane = lax.broadcasted_iota(jnp.int32, shape, 2) // rank
    own = (owner == lane).reshape(2 * pairs * tile, QUAD * rank)
    for quad in range(slots // tile):
        both = lowered_ref[:, quad * tile : (quad + 1) * tile, :].reshape(pairs * tile, wide)
        weight = weight_ref[quad * QUAD : (quad + 1) * QUAD].reshape(QUAD * rank, columns)
        lowered = jnp.concatenate([both[:, :rank], both[:, rank:]], axis=0)
        spread = jnp.where(own, jnp.concatenate([lowered] * QUAD, axis=-1), 0)
        update = jnp.dot(spread.astype(BF16), weight, preferred_element_type=F32).astype(BF16)
        update = update.reshape(2, pairs, tile, columns)
        for half in range(2):
            out_ref[:, half, quad * tile : (quad + 1) * tile, :] = update[half]


def raise_rank(lowered, weight):
    pairs, slots, wide = lowered.shape
    columns = weight.shape[2]
    return call(
        up_kernel,
        jax.ShapeDtypeStruct((pairs, 2, slots, columns), BF16),
        (lowered, weight),
        pairs * 2 * slots * columns * wide * QUAD,
        name="up",
    )


def as_column(row):
    return jnp.transpose(jnp.broadcast_to(row, (8, row.shape[1])))[:, 0:1]


def prepare_kernel(slots_ref, accepted_ref, base_ref, take_ref, base_out):
    count, places = take_ref.shape
    rows = base_ref.shape[0]
    mine = lax.broadcasted_iota(jnp.int32, (count, rows), 1) == as_column(accepted_ref[...])
    slot = jnp.sum(jnp.where(mine, slots_ref[...], 0), axis=1, keepdims=True)
    place = lax.broadcasted_iota(jnp.int32, (count, places), 1)
    take_ref[...] = jnp.where(place == slot, 1.0, 0.0).astype(BF16)
    base_out[...] = jnp.dot(
        jnp.where(mine, 1.0, 0.0),
        base_ref[...],
        preferred_element_type=F32,
        precision=lax.Precision.HIGHEST,
    )


def choose_kernel(take_ref, returned_ref, base_ref, chosen_ref):
    update = jnp.dot(take_ref[...], returned_ref[...], preferred_element_type=F32)
    chosen_ref[...] = (base_ref[...] + update).astype(BF16)


def finish_kernel(slots_ref, returned_ref, base_ref, out_ref):
    rows = out_ref.shape[0]
    places = returned_ref.shape[0]
    column = as_column(slots_ref[...])
    block = 256
    total = base_ref[...]
    place = numbers(lax.broadcasted_iota(jnp.int32, (rows, block), 1))
    for first in range(0, places, block):
        take = one_hot(place == numbers(column - first))
        total += jnp.dot(
            take, returned_ref[first : first + block], preferred_element_type=F32
        )
    out_ref[...] = total.astype(BF16)


def cache_kernel(targets_ref, moved_ref, out_ref):
    count = targets_ref.shape[1]
    place = lax.broadcasted_iota(jnp.int32, (out_ref.shape[0], count), 0)
    take = jnp.where(place == targets_ref[...], 1.0, 0.0).astype(BF16)
    out_ref[...] = jnp.dot(take, moved_ref[...], preferred_element_type=F32).astype(BF16)


def exchange(array, axis, among=None):
    return lax.all_to_all(
        array, axis, split_axis=0, concat_axis=0, tiled=True, axis_index_groups=among
    )


def sum_over_tensor(partial, core, pairs, chips):
    both = lax.all_gather(partial, "tensor", axis=0, axis_index_groups=pairs)
    half = partial.shape[0] // 2
    mine = lax.dynamic_slice_in_dim(both, core * half, half, axis=1).astype(F32)
    mine = (mine[0] + mine[1]).astype(BF16)
    pieces = exchange(mine, "tensor", chips)
    pieces = pieces.reshape(half, 1, *partial.shape[1:])
    summed = jnp.sum(pieces.astype(F32), axis=0).astype(BF16)
    summed = jnp.broadcast_to(summed, (half, *partial.shape[1:]))
    mine = exchange(summed, "tensor", chips)
    return lax.all_gather(mine, "tensor", axis=0, axis_index_groups=pairs, tiled=True)


def per_device(
    tokens,
    row_adapter_index,
    adapter_down_weight,
    adapter_up_weight,
    key_value_weight,
    accepted_branch_rows,
    owner_cache_slots,
):
    owners, groups = lax.axis_size("adapter"), lax.axis_size("tensor")
    rows, features = tokens.shape
    columns = adapter_up_weight.shape[2]
    resident = adapter_down_weight.shape[0]
    here = resident * CAP

    core = lax.rem(lax.axis_index("tensor"), 2)
    pairs = [[2 * y, 2 * y + 1] for y in range(groups // 2)]
    chips = [[2 * y + c for y in range(groups // 2)] for c in range(2)]

    slots, packed = pack(row_adapter_index.reshape(1, rows), tokens)
    received = exchange(packed.reshape(owners, here, features), "adapter")

    tokens, slots = lax.optimization_barrier((tokens, slots))
    received, down_weight, base = sum_base(
        tokens,
        key_value_weight,
        columns,
        groups,
        received,
        jnp.swapaxes(adapter_down_weight, 1, 2),
    )

    partial_rank = lower(received, down_weight)
    lowered = sum_over_tensor(partial_rank, core, pairs, chips)
    update = raise_rank(lowered, adapter_up_weight)
    returned = exchange(update.reshape(owners, here, columns), "adapter")
    base = sum(part.astype(F32) for part in base)
    accepted = accepted_branch_rows.reshape(1, -1)
    count = accepted.shape[1]
    take, base_chosen = call(
        prepare_kernel,
        [
            jax.ShapeDtypeStruct((count, owners * here), BF16),
            jax.ShapeDtypeStruct((count, columns), F32),
        ],
        (slots, accepted, base),
        2 * count * rows * columns,
        name="prepare",
    )
    returned = returned.reshape(owners * here, columns)
    chosen = call(
        choose_kernel,
        jax.ShapeDtypeStruct((count, columns), BF16),
        (take, returned, base_chosen),
        2 * count * owners * here * columns,
        name="choose",
    )
    moved = exchange(chosen.reshape(owners, -1, columns), "adapter").reshape(-1, columns)
    returned, chosen = lax.optimization_barrier((returned, chosen))
    key_value = call(
        finish_kernel,
        jax.ShapeDtypeStruct((rows, columns), BF16),
        (slots, returned, base),
        2 * rows * owners * here * columns,
        name="finish",
    )
    decode_cache = call(
        cache_kernel,
        jax.ShapeDtypeStruct((moved.shape[0], columns), BF16),
        (owner_cache_slots.reshape(1, -1), moved),
        2 * count * count * columns,
        name="cache",
    )
    return (key_value, decode_cache)


def solution(mesh):
    in_specs = (
        P("adapter", "tensor"),
        P("adapter", None),
        P("adapter", "tensor", None),
        P("adapter", None, "tensor"),
        P("tensor", None),
        P("adapter", None, None),
        P(None, "adapter", None),
    )
    out_specs = (P("adapter", "tensor"), P("adapter", "tensor"))
    return jax.shard_map(
        per_device, mesh=mesh, in_specs=in_specs, out_specs=out_specs, check_vma=False
    )
```
